128 devices in a mesh: ctx: 16 (over z, y), mp: 8 (over x, core).
Axes of the slice: x: 4, y: 4, z: 4, core: 2. Of those that a mesh axis runs over, the one named last changes fastest.
Arguments:
- ssd_x: bfloat16 [4096, 16384], P('ctx', 'mp'), may hold values from -6 to 6
- ssd_b: bfloat16 [4096, 128], P('ctx'), may hold values from -0.80078125 to 0.80078125
- ssd_c: bfloat16 [4096, 128], P('ctx'), may hold values from -0.80078125 to 0.80078125
- dt_steps: float32 [64, 4096], P('mp', 'ctx'), may hold values from 0 to 0.6, as said below
- decay_rate: float32 [64], P('mp'), may hold values from 0.5 to 2
- skip_gain: float32 [64], P('mp'), may hold values from 0.5 to 1.5
- doc_ids: int32 [4096], P('ctx'), may hold values from 0 to 3, never falling along the last dimension, each value on 1 to 2048 neighbouring positions
- queries: bfloat16 [4096, 8192], P('ctx', 'mp'), may hold values from -4.5 to 4.5
- key_rows: bfloat16 [4096, 1024], P('ctx', 'mp'), may hold values from -4.5 to 4.5
- values: bfloat16 [4096, 1024], P('ctx', 'mp'), may hold values from -6 to 6
- log_scale: float32 [64], P('mp'), may hold values from 0.05 to 0.15
- moe_in: bfloat16 [4096, 8192], P('ctx', 'mp'), may hold values from -6 to 6
- expert_ids: int32 [4096, 2], P('ctx'), may hold values from 0 to 15, as said below
- route_weights: float32 [4096, 2], P('ctx'), may hold values from 0.1 to 0.9
- w_gate: bfloat16 [8, 8192, 6144], P('mp', None, 'ctx'), may hold values from -0.0625 to 0.0625
- w_up: bfloat16 [8, 8192, 6144], P('mp', None, 'ctx'), may hold values from -0.0625 to 0.0625
- w_down: bfloat16 [8, 6144, 8192], P('mp', 'ctx'), may hold values from -0.0546875 to 0.0546875
Outputs:
- ssd_out: bfloat16 [4096, 16384], P('ctx', 'mp')
- attn_out: bfloat16 [4096, 8192], P('ctx', 'mp')
- moe_out: bfloat16 [4096, 8192], P('ctx', 'mp')
The draws below stay inside these ranges and needn't reach their ends.
Inputs may be any that keep to these rules, and one draw needn't show every extreme that they name: `dt_steps`: Positive. `expert_ids`: each row names two different experts. In every aligned block of 256 rows (the tokens of one index of ctx) each of the 16 experts is named by exactly 32 rows, and the experts fall into two sets of 8 such that every row of the block names one of each set.
All inputs are finite; a program needn't handle non-finite values.
Results may differ from the reference program's by a relative error of at most 0.02.
Values may be sent and summed in bfloat16 or wider, within the bound.
A program may use at most 128 MiB of HBM per device.

```python
import math
import jax
import jax.numpy as jnp
import numpy as np
from jax import lax

D = 8192
FF = 12288
HEADS = 64
KV_HEADS = 8
HEAD_DIM = 128
SSD_HEADS = 64
SSD_DIM = 256
STATES = 128
EXPERTS = 16
HELD = 4
SEG = 128
DOCS = 4
TOK_SHARD = 256
PACKED_SPAN = 4096
CAP = 32
PART = 6144
FDEV = 384
N_CTX = 16
N_MP = 8


def draw_dt_steps(key, part):
    key = jax.random.fold_in(key, 7)
    stochastic_seed_list = jax.random.split(key, 7)
    quick_share = 0.5
    quick = jax.random.uniform(stochastic_seed_list[0], (SSD_HEADS, 1)) < quick_share
    fast_rate = jax.random.uniform(stochastic_seed_list[1], (SSD_HEADS, 1), minval=1.0 / 50, maxval=1.0 / 30)
    slow_rate = jax.random.uniform(stochastic_seed_list[2], (SSD_HEADS, 1), minval=0.1, maxval=0.3) / PACKED_SPAN
    base_rate = jnp.where(quick, fast_rate, slow_rate)
    rough = jnp.exp(jax.random.uniform(stochastic_seed_list[3], (SSD_HEADS, PACKED_SPAN), minval=math.log(0.7), maxval=math.log(1.4)))
    shard_factor = jnp.exp(jax.random.uniform(stochastic_seed_list[4], (SSD_HEADS, PACKED_SPAN // TOK_SHARD, 1), minval=math.log(0.6), maxval=math.log(1.5)))
    shard_factor = jnp.broadcast_to(shard_factor, (SSD_HEADS, PACKED_SPAN // TOK_SHARD, TOK_SHARD)).reshape(SSD_HEADS, PACKED_SPAN)
    sequence_clusters = jax.random.randint(stochastic_seed_list[5], (2,), 0, PACKED_SPAN)
    blend_coefficient = jax.random.uniform(stochastic_seed_list[6], (SSD_HEADS, 2), minval=0.3, maxval=0.5)
    accelerator_slots = jnp.arange(PACKED_SPAN)[None, :]
    surplus_quantity = blend_coefficient[:, 0:1] * (accelerator_slots == sequence_clusters[0]) + blend_coefficient[:, 1:2] * (accelerator_slots == sequence_clusters[1])
    return (base_rate * rough * shard_factor + surplus_quantity).astype(jnp.float32)


def draw_queries(key, part):
    key = jax.random.fold_in(key, 11)
    return jnp.clip(jax.random.normal(key, (PACKED_SPAN, HEADS * HEAD_DIM)), -4.5, 4.5).astype(jnp.bfloat16)


def draw_key_rows(key, part):
    key = jax.random.fold_in(key, 13)
    return jnp.clip(jax.random.normal(key, (PACKED_SPAN, KV_HEADS * HEAD_DIM)), -4.5, 4.5).astype(jnp.bfloat16)


def draw_expert_ids(key, part):
    key = jax.random.fold_in(key, 5)
    capacity = 2 * TOK_SHARD // EXPERTS
    ordered = jnp.arange(2 * TOK_SHARD, dtype=jnp.int32) // capacity

    def one_block(block_key):
        relabel_key, order_key, flip_key = jax.random.split(block_key, 3)
        relabel = jax.random.permutation(relabel_key, EXPERTS).astype(jnp.int32)
        order = jax.random.permutation(order_key, TOK_SHARD)
        paired = jnp.stack([ordered[:TOK_SHARD], ordered[TOK_SHARD:]], axis=1)[order]
        paired = relabel[paired]
        flipped = jax.random.randint(flip_key, (TOK_SHARD, 1), 0, 2)
        return jnp.where(flipped == 1, paired[:, ::-1], paired)
    block_keys = jax.random.split(key, PACKED_SPAN // TOK_SHARD)
    return jax.vmap(one_block)(block_keys).reshape(PACKED_SPAN, 2).astype(jnp.int32)


def block_scale(own_key, shape, shards, low, high):
    def one(dim, shards_of):
        draws = jax.random.uniform(jax.random.fold_in(jax.random.fold_in(own_key, 6), dim), (shards_of,), jnp.float32, low / len(shards), high / len(shards))
        return jnp.repeat(jnp.exp(draws), shape[dim] // shards_of).reshape((-1,) + (1,) * (len(shape) - dim - 1))

    factor_of = one(*shards[0])
    for cut in shards[1:]:
        factor_of = factor_of * one(*cut)
    return factor_of


def profile(count, total, most, lean):
    portions = [(1 << 20) // math.isqrt(standing ** lean) + 1 for standing in range(2, count + 1)]
    rest, given = total - most - (count - 1), [1] * (count - 1)
    while rest > 0:
        free = [i for i in range(count - 1) if given[i] < most]
        mass, left = sum([portions[i] for i in free]), rest
        for i in free:
            more = min(most - given[i], max(1, left * portions[i] // mass), rest)
            given[i] = given[i] + more
            rest = rest - more
    return np.array([most] + given)


def uneven_parts(rng, number_of, total, most, lean):
    if number_of == 2:
        one = jax.random.randint(rng, (), max(1, total - most), min(most, total - 1) + 1)
        return jnp.stack([one, total - one])
    sizes = jnp.asarray(profile(number_of, total, most, lean), jnp.int32)
    couples = (number_of - 1) // 2
    donor, receiver = sizes[1:1 + 2 * couples:2], sizes[2:2 + 2 * couples:2]
    slack = jnp.minimum(donor - 1, most - receiver)
    passed = jax.random.randint(jax.random.fold_in(rng, 1), (couples,), 0, 1 << 20) % (slack + 1)
    sizes = sizes.at[1:1 + 2 * couples:2].set(donor - passed).at[2:2 + 2 * couples:2].set(receiver + passed)
    return sizes[jax.random.permutation(jax.random.fold_in(rng, 2), number_of)]


def centred(stream_key, extent, spread, limit, pieces=(), held_as=jnp.bfloat16):
    entries = jax.random.normal(stream_key, extent, jnp.float32) * spread
    if len(pieces) > 0:
        entries = block_scale(stream_key, extent, pieces, -0.22, 0.18) * entries
    return jnp.clip(entries, min=-limit, max=limit).astype(held_as)


def setup_inputs(seed: int = 0) -> dict:
    seeds = jax.random.split(jax.random.key(seed), 18)
    ssd_x = centred(seeds[0], (PACKED_SPAN, SSD_HEADS * SSD_DIM), 1.0, 6.0, ((0, 16), (1, 8)))
    ssd_b = centred(seeds[1], (PACKED_SPAN, STATES), (0.45 / STATES ** 0.25), 0.80078125, ((0, 16),))
    ssd_c = centred(seeds[2], (PACKED_SPAN, STATES), (0.45 / STATES ** 0.25), 0.80078125, ((0, 16),))
    dt_steps = draw_dt_steps(jax.random.fold_in(seeds[17], 71), 0)
    decay_rate = jnp.clip(jnp.exp(math.log(2.0) - 1.3862944 * jax.random.uniform(seeds[4], (SSD_HEADS,), jnp.float32) ** block_scale(seeds[4], (SSD_HEADS,), ((0, 8),), -0.2, 0.2)), 0.5, 2.0)
    skip_gain = jnp.clip(0.5 + 1.0 * jax.random.uniform(seeds[5], (SSD_HEADS,), jnp.float32) ** block_scale(seeds[5], (SSD_HEADS,), ((0, 8),), -0.2, 0.2), 0.5, 1.5)
    doc_ids = jnp.searchsorted(jnp.cumsum(uneven_parts(seeds[6], DOCS, PACKED_SPAN, PACKED_SPAN // 2, 0)), jnp.arange(PACKED_SPAN), side="right").astype(jnp.int32)
    queries = draw_queries(jax.random.fold_in(seeds[17], 71), 0)
    key_rows = draw_key_rows(jax.random.fold_in(seeds[17], 71), 0)
    values = centred(seeds[9], (PACKED_SPAN, KV_HEADS * HEAD_DIM), 1.0, 6.0, ((0, 16), (1, 8)))
    log_scale = jnp.clip(jnp.exp(math.log(0.15) - 1.0986123 * jax.random.uniform(seeds[10], (HEADS,), jnp.float32) ** block_scale(seeds[10], (HEADS,), ((0, 8),), -0.2, 0.2)), 0.05, 0.15)
    moe_in = centred(seeds[11], (PACKED_SPAN, D), 1.0, 6.0, ((0, 16), (1, 8)))
    expert_ids = draw_expert_ids(jax.random.fold_in(seeds[17], 71), 0)
    route_weights = jnp.clip(0.1 + 0.79999997 * jax.random.uniform(seeds[13], (PACKED_SPAN, 2), jnp.float32) ** block_scale(seeds[13], (PACKED_SPAN, 2), ((0, 16),), -0.2, 0.2), 0.1, 0.9)
    w_gate = centred(seeds[14], (N_MP, D, PART), D ** -0.5, 0.0625, ((0, 8), (2, 16)))
    w_up = centred(seeds[15], (N_MP, D, PART), D ** -0.5, 0.0625, ((0, 8), (2, 16)))
    w_down = centred(seeds[16], (N_MP, PART, D), FF ** -0.5, 0.0546875, ((0, 8), (1, 16)))
    return dict(ssd_x=ssd_x, ssd_b=ssd_b, ssd_c=ssd_c, dt_steps=dt_steps, decay_rate=decay_rate, skip_gain=skip_gain, doc_ids=doc_ids, queries=queries, key_rows=key_rows, values=values, log_scale=log_scale, moe_in=moe_in, expert_ids=expert_ids, route_weights=route_weights, w_gate=w_gate, w_up=w_up, w_down=w_down)


def settle(array):
    return lax.optimization_barrier(array.astype(jnp.bfloat16)).astype(jnp.float32)

def ssd_layer(ssd_x, ssd_b, ssd_c, dt_steps, decay_rate, skip_gain, doc_ids):
    blocks = PACKED_SPAN // SEG
    x_blocks = ssd_x.reshape(blocks, SEG, SSD_HEADS, SSD_DIM)
    b_blocks = ssd_b.reshape(blocks, SEG, STATES)
    c_blocks = ssd_c.reshape(blocks, SEG, STATES)
    log_decay = -(dt_steps * decay_rate[:, None])
    decay_blocks = log_decay.reshape(SSD_HEADS, blocks, SEG).transpose(1, 0, 2)
    doc_blocks = doc_ids.reshape(blocks, SEG)
    causal = jnp.arange(SEG)[:, None] >= jnp.arange(SEG)[None, :]

    def advance(running, block_item):
        carried_state, last_doc = running
        input_local, b_here, c_here, decay_here, doc_here = block_item
        cumulative = jnp.cumsum(decay_here, axis=1)
        linked = (doc_here[:, None] == doc_here[None, :]) & causal
        inner_prod = jnp.dot(c_here, b_here.T, preferred_element_type=jnp.float32)
        decay_gaps = cumulative[:, :, None] - cumulative[:, None, :]
        decay_mask = jnp.where(linked[None], jnp.exp(jnp.where(linked[None], decay_gaps, 0.0)), 0.0)
        weights = settle(inner_prod[None] * decay_mask)
        block_term = jnp.einsum('hts,shp->thp', weights, input_local.astype(jnp.float32))
        leading_document = doc_here[0]
        end_doc = doc_here[-1]
        carried_flag = (last_doc == leading_document).astype(jnp.float32)
        entering = carried_state * carried_flag
        entering_low = settle(entering)
        carried_term = jnp.einsum('tn,hpn->thp', c_here.astype(jnp.float32), entering_low)
        lifting = jnp.exp(cumulative) * (doc_here == leading_document).astype(jnp.float32)[None, :]
        carried_term = carried_term * lifting.T[:, :, None]
        result = block_term + carried_term + skip_gain[None, :, None] * input_local.astype(jnp.float32)
        tail_fade = jnp.where((doc_here == end_doc)[None, :], jnp.exp(cumulative[:, -1:] - cumulative), 0.0)
        scaled = settle(input_local.astype(jnp.float32) * tail_fade.T[:, :, None])
        local_state = jnp.einsum('shp,sn->hpn', scaled, b_here.astype(jnp.float32))
        block_decay = jnp.exp(cumulative[:, -1]) * (leading_document == end_doc).astype(jnp.float32)
        next_state = block_decay[:, None, None] * entering + local_state
        return ((next_state, end_doc), result.astype(jnp.bfloat16))
    start_state = (jnp.zeros((SSD_HEADS, SSD_DIM, STATES), jnp.float32), jnp.array(-1, dtype=doc_ids.dtype))
    unused, outputs = lax.scan(advance, start_state, (x_blocks, b_blocks, c_blocks, decay_blocks, doc_blocks))
    return outputs.reshape(PACKED_SPAN, SSD_HEADS * SSD_DIM)

def attention(queries, key_rows, values, log_scale, doc_ids):
    ratio = HEADS // KV_HEADS
    q_heads = queries.reshape(PACKED_SPAN, HEADS, HEAD_DIM)
    k_heads = key_rows.reshape(PACKED_SPAN, KV_HEADS, HEAD_DIM)
    v_heads = values.reshape(PACKED_SPAN, KV_HEADS, HEAD_DIM)
    accelerator_slots = jnp.arange(PACKED_SPAN)
    allowed = (accelerator_slots[:, None] >= accelerator_slots[None, :]) & (doc_ids[:, None] == doc_ids[None, :])
    growth = jnp.log1p(accelerator_slots.astype(jnp.float32))

    def one_head(head_index):
        shared = head_index // ratio
        query = lax.dynamic_index_in_dim(q_heads, head_index, 1, keepdims=False)
        key_head = lax.dynamic_index_in_dim(k_heads, shared, 1, keepdims=False)
        value_head = lax.dynamic_index_in_dim(v_heads, shared, 1, keepdims=False)
        raw = jnp.dot(query, key_head.T, preferred_element_type=jnp.float32)
        stretch = (1.0 + log_scale[head_index] * growth) / math.sqrt(HEAD_DIM)
        scores = jnp.where(allowed, raw * stretch[:, None], -1e+30)
        peak = lax.optimization_barrier(jnp.max(scores, axis=1, keepdims=True))
        probs = jnp.where(allowed, jnp.exp(scores - peak), 0.0)
        totals = lax.optimization_barrier(jnp.sum(probs, axis=1, keepdims=True))
        mixed = jnp.dot(probs.astype(jnp.bfloat16), value_head, preferred_element_type=jnp.float32) / totals
        return mixed.astype(jnp.bfloat16)
    outputs = lax.map(one_head, jnp.arange(HEADS))
    return outputs.transpose(1, 0, 2).reshape(PACKED_SPAN, HEADS * HEAD_DIM)

def expert_layer(moe_in, expert_ids, route_weights, w_gate, w_up, w_down):
    group = N_MP // HELD
    routed = N_CTX * CAP

    def add_expert(expert, total):
        matches = expert_ids == expert
        shares = lax.optimization_barrier(jnp.sum(jnp.where(matches, route_weights, 0.0), axis=1))
        named = jnp.any(matches, axis=1)
        chosen = jnp.nonzero(named, size=routed)[0].astype(jnp.int32)
        features = moe_in[chosen]

        def add_owner(member, summed):
            owner = expert * group + member
            gate_cols = lax.dynamic_index_in_dim(w_gate, owner, 0, keepdims=False)
            up_cols = lax.dynamic_index_in_dim(w_up, owner, 0, keepdims=False)
            down_rows = lax.dynamic_index_in_dim(w_down, owner, 0, keepdims=False)
            gate = jnp.dot(features, gate_cols, preferred_element_type=jnp.float32)
            upward = jnp.dot(features, up_cols, preferred_element_type=jnp.float32)
            hidden = (jax.nn.silu(gate) * upward).astype(jnp.bfloat16)

            def add_part(segment_ordinal, partial_value):
                piece = lax.dynamic_slice_in_dim(hidden, segment_ordinal * FDEV, FDEV, 1)
                rows_here = lax.dynamic_slice_in_dim(down_rows, segment_ordinal * FDEV, FDEV, 0)
                return partial_value + settle(jnp.dot(piece, rows_here, preferred_element_type=jnp.float32))
            return lax.fori_loop(0, N_CTX, add_part, summed)
        output = lax.fori_loop(0, group, add_owner, jnp.zeros((routed, D), jnp.float32))
        return total.at[chosen].add(output * shares[chosen][:, None])
    total = lax.fori_loop(0, HELD, add_expert, jnp.zeros((PACKED_SPAN, D), jnp.float32))
    return total.astype(jnp.bfloat16)

def reference(ssd_x, ssd_b, ssd_c, dt_steps, decay_rate, skip_gain, doc_ids, queries, key_rows, values, log_scale, moe_in, expert_ids, route_weights, w_gate, w_up, w_down):
    ssd_out = ssd_layer(ssd_x, ssd_b, ssd_c, dt_steps, decay_rate, skip_gain, doc_ids)
    attn_out = attention(queries, key_rows, values, log_scale, doc_ids)
    moe_out = expert_layer(moe_in, expert_ids, route_weights, w_gate, w_up, w_down)
    return (ssd_out, attn_out, moe_out)
```

```python
import math

import jax
import jax.numpy as jnp
from jax import lax
from jax.experimental import pallas as pl
from jax.experimental.pallas import tpu as pltpu
from jax.sharding import PartitionSpec as P

HEAD_DIM = 128
HELD = 4
SEG = 128
CAP = 32
WINDOW = 8
LOG2E = math.log2(math.e)
MESH = pl.DeviceIdType.MESH
F32 = jnp.float32
BF16 = jnp.bfloat16
HIGH = lax.Precision.HIGHEST


def dot(a, b, precision=None):
    return jnp.dot(a, b, preferred_element_type=F32, precision=precision)


def dot_nt(a, b, precision=None):
    return lax.dot_general(
        a, b, (((1,), (1,)), ((), ())), preferred_element_type=F32, precision=precision
    )


def iota(shape, dim):
    return lax.broadcasted_iota(jnp.int32, shape, dim)


def kernel(
    x_ref, b_ref, c_ref, ld_ref, skip_ref, docr_ref, docc_ref, q_ref, kv_ref, st_ref,
    moe_ref, ids_ref, rw_ref, wg_ref, wu_ref, wd_ref,
    ssd_out, attn_out, moe_out,
    wgu, wd, xs, pk, ptt, share, pl_land, l1, l2, qs, l3, l4, rx, fin, gu, hid,
    kv, sb, sl, en, er, t0s, ys, m_s, l_s, acc_s,
    w_sem, own_sem,
    xa_s, xa_r, sm_s, sm_r, bg_s, bg_r, bf_s, bf_r, cx_s, cx_r,
    cd_s, cd_r, ra_s, ra_r, rb_s, rb_r, xb_s, xb_r,
    kv_s, kv_r, sa_s, sa_r, se_s, se_r,
):
    c = lax.axis_index("ctx")
    m = lax.axis_index("mp")
    z, y = c // 4, c % 4
    x, g = m // 2, m % 2
    sib = {"ctx": c, "mp": x * 2 + (1 - g)}

    def zy(zz, yy):
        return {"ctx": (zz % 4) * 4 + yy % 4, "mp": m}

    def xdev(xx):
        return {"ctx": c, "mp": (xx % 4) * 2 + g}

    def ctx(cc):
        return {"ctx": cc % 16, "mp": m}

    def remote(src, dst, s, r, dev):
        return pltpu.make_async_remote_copy(
            src_ref=src, dst_ref=dst, send_sem=s, recv_sem=r, device_id=dev, device_id_type=MESH
        )

    loads = [
        pltpu.make_async_copy(wg_ref.at[0], wgu.at[:, pl.ds(0, 384)], w_sem.at[0]),
        pltpu.make_async_copy(wu_ref.at[0], wgu.at[:, pl.ds(384, 384)], w_sem.at[1]),
        pltpu.make_async_copy(wd_ref.at[0], wd, w_sem.at[2]),
    ]
    for load in loads:
        load.start()

    bar = pltpu.get_barrier_semaphore()
    for k in range(1, 16):
        pl.semaphore_signal(bar, inc=1, device_id=ctx(c + k), device_id_type=MESH)
    for k in range(1, 4):
        pl.semaphore_signal(bar, inc=1, device_id=xdev(x + k), device_id_type=MESH)
    pl.semaphore_signal(bar, inc=1, device_id=sib, device_id_type=MESH)

    expert = iota((8, 256), 0)
    ids0, ids1 = ids_ref[0:1, :], ids_ref[1:2, :]
    named = ((ids0 == expert) | (ids1 == expert)).astype(F32)
    weight = jnp.where(ids0 == expert, rw_ref[0:1, :], 0.0) + jnp.where(
        ids1 == expert, rw_ref[1:2, :], 0.0
    )
    upto = (iota((256, 256), 0) <= iota((256, 256), 1)).astype(BF16)
    rank = dot(named.astype(BF16), upto).astype(jnp.int32) - 1
    slot = iota((CAP, 256), 0)
    for e in range(HELD):
        place = jnp.where((rank[e : e + 1, :] == slot) & (named[e : e + 1, :] > 0.0), 1.0, 0.0)
        pk[e] = dot(place.astype(BF16), moe_ref[...]).astype(BF16)
        share[pl.ds(e * CAP, CAP), :] = jnp.broadcast_to(
            jnp.sum(place * weight[e : e + 1, :], axis=1, keepdims=True), (CAP, 128)
        )
        ptt[pl.ds(e * CAP, CAP), :] = place

    pl.semaphore_wait(bar, 19)

    xa = []
    for k in range(1, 4):
        cp = remote(
            pk.at[(x + k) % 4], xs.at[g, x, z, y], xa_s.at[k - 1], xa_r.at[k - 1], xdev(x + k)
        )
        cp.start()
        xa.append(cp)
    own = pltpu.make_async_copy(pk.at[x], xs.at[g, x, z, y], own_sem.at[0])
    own.start()
    kv0 = pltpu.make_async_copy(kv_ref, kv.at[0], own_sem.at[1])
    kv0.start()

    low = iota((SEG, SEG), 0) >= iota((SEG, SEG), 1)
    tri = low.astype(F32)
    cum_r, cum_c, inner, linked, bt = [], [], [], [], []
    for k in range(2):
        rows = slice(k * SEG, (k + 1) * SEG)
        ld = ld_ref[:, rows]
        cum_r.append(dot_nt(ld, tri, HIGH))
        cum_c.append(dot_nt(tri, ld, HIGH))
        inner.append(dot_nt(c_ref[rows, :], b_ref[rows, :]))
        linked.append((docc_ref[rows, :] == docr_ref[0:1, rows]) & low)
        bt.append(b_ref[rows, :].astype(F32).T)
    first = [docr_ref[:, k * SEG : k * SEG + 1] for k in range(2)]
    last = [docr_ref[:, k * SEG + SEG - 1 : (k + 1) * SEG] for k in range(2)]
    dec = [
        jnp.exp(cum_r[k][:, SEG - 1 : SEG]) * (first[k] == last[k]).astype(F32) for k in range(2)
    ]
    tail = [
        jnp.where(
            docr_ref[:, k * SEG : (k + 1) * SEG] == last[k],
            jnp.exp(cum_r[k][:, SEG - 1 : SEG] - cum_r[k]),
            0.0,
        )
        for k in range(2)
    ]
    lift = [
        jnp.exp(cum_c[k])
        * (docc_ref[k * SEG : (k + 1) * SEG, 0:8] == first[k][0:1, :]).astype(F32)
        for k in range(2)
    ]
    joined = (last[0] == first[1]).astype(F32)
    whole = dec[1] * joined * dec[0]

    def head_states(h):
        cols = slice(h * 256, (h + 1) * 256)
        locs = []
        for k in range(2):
            rows = slice(k * SEG, (k + 1) * SEG)
            xb = x_ref[rows, cols]
            locs.append(dot((bt[k] * tail[k][h : h + 1, :]).astype(BF16), xb))
        t0s[h] = locs[0]
        total = locs[1] + (dec[1] * joined)[h : h + 1, :] * locs[0]
        row = iota((16, 128), 0)
        w = jnp.broadcast_to(whole[h : h + 1, :], (16, 128))
        w_hi = w.astype(BF16).astype(F32)
        info = jnp.where(
            row == 0,
            w_hi,
            jnp.where(
                row == 1,
                w - w_hi,
                jnp.where(row == 2, first[0][0:1, :], last[1][0:1, :]),
            ),
        ).astype(BF16)
        for half in range(2):
            sb[2 * h + half, pl.ds(0, 128), :] = total[:, half * 128 : half * 128 + 128].astype(
                BF16
            )
            sb[2 * h + half, pl.ds(128, 16), :] = info

    def head_inside(h):
        cols = slice(h * 256, (h + 1) * 256)
        for k in range(2):
            rows = slice(k * SEG, (k + 1) * SEG)
            xb = x_ref[rows, cols]
            gap = cum_c[k][:, h : h + 1] - cum_r[k][h : h + 1, :]
            w = jnp.where(linked[k], inner[k] * jnp.exp(jnp.where(linked[k], gap, 0.0)), 0.0)
            ys[rows, cols] = dot(w.astype(BF16), xb) + skip_ref[h] * xb.astype(F32)

    for h in range(4):
        head_states(h)

    own.wait()
    for cp in xa:
        cp.wait()

    def xv(h, j, i, k):
        cols = pl.ds(2 * h, 2) if j is None else 2 * h + j
        return xs.at[g, cols, i % 4, k % 4] if h == 0 else xs.at[g, cols, k % 4, i % 4]

    big = (z, y)
    small = (y, z)

    def big_dev(h, d):
        return zy(z + d, y) if h == 0 else zy(z, y + d)

    def small_dev(h, d):
        return zy(z, y + d) if h == 0 else zy(z + d, y)

    order = (0, -1, 1, 2)

    def cp_small(h, d):
        v = xv(h, None, big[h], small[h])
        n = 0 if d == 1 else 1
        return remote(v, v, sm_s.at[h, n], sm_r.at[h, n], small_dev(h, d))

    def cp_small_fwd(h, d):
        n, j = (2, 0) if d == 1 else (3, 1)
        v = xv(h, j, big[h], small[h] - d + 4)
        return remote(v, v, sm_s.at[h, n], sm_r.at[h, n], small_dev(h, d))

    def cp_big(h, d, r):
        n = 0 if d == 1 else 1
        v = xv(h, None, big[h], small[h] + order[r] + 4)
        return remote(v, v, bg_s.at[h, n, r], bg_r.at[h, n, r], big_dev(h, d))

    def cp_big_fwd(h, d, r):
        n = 0 if d == 1 else 1
        v = xv(h, n, big[h] - d + 4, small[h] + order[r] + 4)
        return remote(v, v, bf_s.at[h, n, r], bf_r.at[h, n, r], big_dev(h, d))

    def cp_cross(h, d):
        i = (big[h] + d + 4) % 4
        cols = pl.ds(2 * h, 2)
        v = xs.at[g, cols, i] if h == 0 else xs.at[g, cols, :, i]
        return remote(v, v, cx_s.at[h, d % 4], cx_r.at[h, d % 4], sib)

    sends = []

    def go(cp):
        cp.start()
        sends.append(cp)

    for h in range(2):
        for d in (1, -1):
            go(cp_small(h, d))
    for h in range(2):
        for d in (1, -1):
            go(cp_big(h, d, 0))

    for h in range(4, 8):
        head_states(h)
    head_inside(0)

    for d, r in ((1, 1), (-1, 2)):
        for h in range(2):
            cp_small(h, d).wait_recv()
            go(cp_small_fwd(h, d))
            for e in (1, -1):
                go(cp_big(h, e, r))
    head_inside(1)
    for h in range(2):
        for d in (1, -1):
            cp_small_fwd(h, d).wait_recv()
        for e in (1, -1):
            go(cp_big(h, e, 3))
        go(cp_cross(h, 0))

    todo = [2, 3, 4, 5, 6, 7]
    for r in range(4):
        for h in range(2):
            for d in (1, -1):
                cp_big(h, d, r).wait_recv()
                go(cp_big_fwd(h, d, r))
        if todo:
            head_inside(todo.pop(0))
            head_inside(todo.pop(0))
    for h in range(2):
        go(cp_cross(h, -1))
        go(cp_cross(h, 1))

    def state_out(k):
        return remote(
            sb.at[(c + k) % 16], sl.at[c], sa_s.at[k], sa_r.at[k], ctx(c + k)
        )

    states = []
    for k in range(1, 16):
        cp = state_out(k)
        cp.start()
        states.append(cp)
    mine = pltpu.make_async_copy(sb.at[c], sl.at[c], own_sem.at[2])
    mine.start()

    kv0.wait()

    def key_out(k):
        return remote(kv.at[0], kv.at[k], kv_s.at[k], kv_r.at[k], ctx(c + k))

    for k in range(1, WINDOW + 1):

        @pl.when(c + k < 16)
        def _():
            key_out(k).start()

    for h in range(2):
        for r in range(4):
            for d in (1, -1):
                cp_big_fwd(h, d, r).wait_recv()
        go(cp_cross(h, 2))
    for cp in sends:
        cp.wait_send()

    def cross_in(h, d):
        i = (big[h] + d + 4) % 4
        cols = pl.ds(2 * h, 2)
        v = xs.at[1 - g, cols, i] if h == 0 else xs.at[1 - g, cols, :, i]
        return remote(v, v, cx_s.at[h, d % 4], cx_r.at[h, d % 4], sib)

    for h in range(2):
        for d in (0, -1, 1, 2):
            cross_in(h, d).wait_recv()
    for load in loads:
        load.wait()

    gu[...] = jnp.zeros_like(gu)

    def gate_up(i, carry):
        gg, xx = i // 4, i % 4
        block = pl.multiple_of((xx * 2 + gg) * 1024, 1024)
        gu[...] += dot(xs[gg, xx].reshape(512, 1024), wgu[pl.ds(block, 1024), :])
        return carry

    lax.fori_loop(0, 8, gate_up, 0)
    gate, up = gu[:, 0:384], gu[:, 384:768]
    hid[...] = (gate / (1.0 + jnp.exp(-gate)) * up).astype(BF16)

    ps, pa = xs.at[0], xs.at[1]

    def cp_down(xx):
        return remote(ps.at[xx], pl_land.at[xx], cd_s.at[xx], cd_r.at[xx], sib)

    for xx in range(4):

        def down_sib(n, carry):
            off = pl.multiple_of(n * 512, 512)
            col = pl.multiple_of((xx * 2 + 1 - g) * 1024 + n * 512, 512)
            r = dot(hid[...], wd[:, pl.ds(col, 512)])
            ps[xx, :, :, :, pl.ds(off, 512)] = r.astype(BF16).reshape(4, 4, CAP, 512)
            return carry

        lax.fori_loop(0, 2, down_sib, 0)
        cp_down(xx).start()

    def pv(h, j, i):
        return pa.at[2 * h + j, i % 4] if h == 0 else pa.at[2 * h + j, :, i % 4]

    def ra_first(h, j):
        d = 1 if j == 0 else -1
        return remote(
            pv(h, j, big[h] + 2), l1.at[h, j], ra_s.at[h, j], ra_r.at[h, j], big_dev(h, d)
        )

    def ra_block(h, j, d):
        n = 0 if d == 1 else 1
        return remote(
            pv(h, j, big[h] + d + 4),
            l2.at[h, n, j],
            ra_s.at[h, 2 + 2 * n + j],
            ra_r.at[h, 2 + 2 * n + j],
            big_dev(h, d),
        )

    for xx in range(4):
        cp_down(xx).wait_recv()

        def down_own(n, carry):
            off = pl.multiple_of(n * 512, 512)
            col = pl.multiple_of((xx * 2 + g) * 1024 + n * 512, 512)
            r = dot(hid[...], wd[:, pl.ds(col, 512)])
            r = r.reshape(4, 4, CAP, 512) + pl_land[xx, :, :, :, pl.ds(off, 512)].astype(F32)
            pa[xx, :, :, :, pl.ds(off, 512)] = r.astype(BF16)
            return carry

        lax.fori_loop(0, 2, down_own, 0)
        h, j = xx // 2, xx % 2
        ra_first(h, j).start()
        ra_block(h, j, -1 if j == 0 else 1).start()

    m_s[...] = jnp.full_like(m_s, -1e30)
    l_s[...] = jnp.zeros_like(l_s)
    acc_s[...] = jnp.zeros_like(acc_s)

    def absorb(k, diagonal):
        keys = kv[k, pl.ds(0, 256), :]
        vals = kv[k, pl.ds(256, 256), :]
        docs = kv[k, pl.ds(512, 16), :].astype(F32)
        doc_row = jnp.concatenate([docs[0:1, :], docs[1:2, :]], axis=1)
        docc = docc_ref[...]
        allowed = jnp.concatenate([docc, docc], axis=1) == doc_row
        if diagonal:
            allowed = allowed & (iota((256, 256), 0) >= iota((256, 256), 1))
        bias = jnp.where(allowed, 0.0, -1e30)
        for h in range(8):
            s = dot_nt(q_ref[:, h * 128 : h * 128 + 128], keys) + bias
            st = st_ref[:, h : h + 1]
            old = m_s[h][:, 0:1]
            new = jnp.maximum(old, jnp.max(s, axis=1, keepdims=True))
            p = jnp.exp2((s - new) * st)
            fade = jnp.exp2((old - new) * st)
            l_s[h] = l_s[h] * fade + jnp.sum(p, axis=1, keepdims=True)
            acc_s[h] = acc_s[h] * fade + dot(p.astype(BF16), vals)
            m_s[h] = jnp.broadcast_to(new, (256, 128))

    def absorb_range(lo, hi):
        def body(k, carry):
            remote(kv.at[0], kv.at[k], kv_s.at[k], kv_r.at[k], ctx(c + k)).wait_recv()
            absorb(k, False)
            return carry

        lax.fori_loop(lo, jnp.maximum(jnp.minimum(c + 1, hi), lo), body, 0)

    absorb(0, True)
    absorb_range(1, 2)

    for h in range(2):
        ra_first(h, 0).wait_recv()
        v = pv(h, 0, big[h] + 1)
        v[...] = (v[...].astype(F32) + l1[h, 0].astype(F32)).astype(BF16)
        ra_block(h, 0, 1).start()
        ra_first(h, 1).wait_recv()
        v = pv(h, 1, big[h] + 3)
        v[...] = (v[...].astype(F32) + l1[h, 1].astype(F32)).astype(BF16)
        ra_block(h, 1, -1).start()

    mine.wait()

    def scan(i, carry):
        state, before = carry

        @pl.when(i != c)
        def _():
            k = (c - i + 16) % 16
            remote(
                sb.at[c], sl.at[i], sa_s.at[k], sa_r.at[k], ctx(c + 1)
            ).wait_recv()

        info = sl[i, pl.ds(128, 16), :].astype(F32)
        entering = jnp.where(before == info[2:3, :], state, 0.0)
        en[i] = entering.astype(BF16)
        state = (info[0:1, :] + info[1:2, :]) * entering + sl[i, pl.ds(0, 128), :].astype(F32)
        return state, info[3:4, :]

    lax.fori_loop(
        0, 16, scan, (jnp.zeros((128, 128), F32), jnp.full((1, 128), -1.0, F32))
    )

    def state_back(k):
        return remote(en.at[(c + k) % 16], er.at[c], se_s.at[k], se_r.at[k], ctx(c + k))

    backs = []
    for k in range(1, 16):
        cp = state_back(k)
        cp.start()
        backs.append(cp)
    mine_back = pltpu.make_async_copy(en.at[c], er.at[c], own_sem.at[3])
    mine_back.start()

    absorb_range(2, 6)

    def rb_first(h, j):
        d = 1 if j == 0 else -1
        return remote(
            qs.at[h, j, (small[h] + 2) % 4],
            l3.at[h, j],
            rb_s.at[h, j],
            rb_r.at[h, j],
            small_dev(h, d),
        )

    def rb_block(h, j, d):
        n = 0 if d == 1 else 1
        return remote(
            qs.at[h, j, (small[h] + d + 4) % 4],
            l4.at[h, n, j],
            rb_s.at[h, 2 + 2 * n + j],
            rb_r.at[h, 2 + 2 * n + j],
            small_dev(h, d),
        )

    for h in range(2):
        for j in range(2):
            for d in (1, -1):
                ra_block(h, j, d).wait_recv()
            qs[h, j] = (
                pv(h, j, big[h])[...].astype(F32)
                + l2[h, 0, j].astype(F32)
                + l2[h, 1, j].astype(F32)
            ).astype(BF16)
            rb_first(h, j).start()
            rb_block(h, j, -1 if j == 0 else 1).start()

    absorb_range(6, 8)

    for h in range(2):
        for j, d in ((0, 1), (1, -1)):
            rb_first(h, j).wait_recv()
            v = qs.at[h, j, (small[h] + d + 4) % 4]
            v[...] = (v[...].astype(F32) + l3[h, j].astype(F32)).astype(BF16)
            rb_block(h, j, d).start()

    absorb_range(8, 9)

    share_x = share[pl.ds(pl.multiple_of(x * CAP, CAP), CAP), 0:1]

    def x_back(k):
        return remote(
            rx.at[(x + k) % 4], fin.at[x], xb_s.at[k - 1], xb_r.at[k - 1], xdev(x + k)
        )

    for h in range(2):
        for j in range(2):
            for d in (1, -1):
                rb_block(h, j, d).wait_recv()
            total = (
                qs[h, j, small[h]].astype(F32)
                + l4[h, 0, j].astype(F32)
                + l4[h, 1, j].astype(F32)
            )
            rx[2 * h + j] = (total * share_x).astype(BF16)
    for k in range(1, 4):
        x_back(k).start()
    own_back = pltpu.make_async_copy(rx.at[x], fin.at[x], own_sem.at[4])
    own_back.start()

    for h in range(8):
        attn_out[:, h * 128 : h * 128 + 128] = (acc_s[h] / l_s[h]).astype(BF16)

    mine_back.wait()
    for cp in backs:
        cp.wait()
    for h in range(8):
        cols = slice(h * 256, (h + 1) * 256)
        e0 = jnp.concatenate([er[2 * h], er[2 * h + 1]], axis=1)
        e1 = (
            joined[h : h + 1, :] * (dec[0][h : h + 1, :] * e0.astype(F32) + t0s[h])
        ).astype(BF16)
        for k, e in ((0, e0), (1, e1)):
            rows = slice(k * SEG, (k + 1) * SEG)
            carried = dot(c_ref[rows, :], e)
            ssd_out[rows, cols] = (ys[rows, cols] + carried * lift[k][:, h : h + 1]).astype(BF16)

    own_back.wait()
    for k in range(1, 4):
        x_back(k).wait()
    moe_out[...] = dot(ptt[...].T.astype(BF16), fin[...].reshape(128, 1024)).astype(BF16)

    for cp in states:
        cp.wait_send()
    for xx in range(4):
        cp_down(xx).wait_send()
    for h in range(2):
        for j in range(2):
            ra_first(h, j).wait_send()
            rb_first(h, j).wait_send()
            for d in (1, -1):
                ra_block(h, j, d).wait_send()
                rb_block(h, j, d).wait_send()
    for k in range(1, WINDOW + 1):

        @pl.when(c + k < 16)
        def _():
            key_out(k).wait_send()


def on_device(
    ssd_x, ssd_b, ssd_c, dt_steps, decay_rate, skip_gain, doc_ids,
    queries, key_rows, values, log_scale,
    moe_in, expert_ids, route_weights, w_gate, w_up, w_down,
):
    positions = ssd_x.shape[0]
    log_decay = -(dt_steps * decay_rate[:, None])
    docs = doc_ids.astype(F32)
    docr = jnp.broadcast_to(docs[None, :], (8, positions))
    docc = jnp.broadcast_to(docs[:, None], (positions, 128))
    kv = jnp.concatenate(
        [
            key_rows,
            values,
            docs.astype(BF16).reshape(2, 128),
            jnp.zeros((30, 128), BF16),
        ],
        axis=0,
    )
    places = lax.axis_index("ctx") * positions + jnp.arange(positions)
    stretch = (
        (1.0 + log_scale[None, :] * jnp.log1p(places.astype(F32))[:, None])
        * (LOG2E / math.sqrt(HEAD_DIM))
    )
    vmem = pl.BlockSpec(memory_space=pltpu.VMEM)
    smem = pl.BlockSpec(memory_space=pltpu.SMEM)
    anyw = pl.BlockSpec(memory_space=pl.ANY)
    dma = pltpu.SemaphoreType.DMA
    return pl.pallas_call(
        kernel,
        out_shape=(
            jax.ShapeDtypeStruct((positions, 2048), BF16),
            jax.ShapeDtypeStruct((positions, 1024), BF16),
            jax.ShapeDtypeStruct((positions, 1024), BF16),
        ),
        in_specs=[vmem] * 4 + [smem] + [vmem] * 8 + [anyw] * 3,
        out_specs=(vmem, vmem, vmem),
        scratch_shapes=[
            pltpu.VMEM((8192, 768), BF16),
            pltpu.VMEM((384, 8192), BF16),
            pltpu.VMEM((2, 4, 4, 4, CAP, 1024), BF16),
            pltpu.VMEM((4, CAP, 1024), BF16),
            pltpu.VMEM((128, 256), F32),
            pltpu.VMEM((128, 128), F32),
            pltpu.VMEM((4, 4, 4, CAP, 1024), BF16),
            pltpu.VMEM((2, 2, 4, CAP, 1024), BF16),
            pltpu.VMEM((2, 2, 2, 4, CAP, 1024), BF16),
            pltpu.VMEM((2, 2, 4, CAP, 1024), BF16),
            pltpu.VMEM((2, 2, CAP, 1024), BF16),
            pltpu.VMEM((2, 2, 2, CAP, 1024), BF16),
            pltpu.VMEM((4, CAP, 1024), BF16),
            pltpu.VMEM((4, CAP, 1024), BF16),
            pltpu.VMEM((512, 768), F32),
            pltpu.VMEM((512, 384), BF16),
            pltpu.VMEM((WINDOW + 1, 544, 128), BF16),
            pltpu.VMEM((16, 144, 128), BF16),
            pltpu.VMEM((16, 144, 128), BF16),
            pltpu.VMEM((16, 128, 128), BF16),
            pltpu.VMEM((16, 128, 128), BF16),
            pltpu.VMEM((8, 128, 256), F32),
            pltpu.VMEM((256, 2048), F32),
            pltpu.VMEM((8, 256, 128), F32),
            pltpu.VMEM((8, 256, 128), F32),
            pltpu.VMEM((8, 256, 128), F32),
            dma((3,)),
            dma((5,)),
            dma((3,)), dma((3,)),
            dma((2, 4)), dma((2, 4)),
            dma((2, 2, 4)), dma((2, 2, 4)),
            dma((2, 2, 4)), dma((2, 2, 4)),
            dma((2, 4)), dma((2, 4)),
            dma((4,)), dma((4,)),
            dma((2, 6)), dma((2, 6)),
            dma((2, 6)), dma((2, 6)),
            dma((3,)), dma((3,)),
            dma((WINDOW + 1,)), dma((WINDOW + 1,)),
            dma((16,)), dma((16,)),
            dma((16,)), dma((16,)),
        ],
        compiler_params=pltpu.CompilerParams(
            collective_id=0, has_side_effects=True, vmem_limit_bytes=60 * 2**20
        ),
        name="layer_pair",
    )(
        ssd_x, ssd_b, ssd_c, log_decay, skip_gain, docr, docc, queries, kv, stretch,
        moe_in, expert_ids.T, route_weights.T, w_gate, w_up, w_down,
    )


def solution(mesh):
    in_specs = (
        P("ctx", "mp"),
        P("ctx", None),
        P("ctx", None),
        P("mp", "ctx"),
        P("mp"),
        P("mp"),
        P("ctx"),
        P("ctx", "mp"),
        P("ctx", "mp"),
        P("ctx", "mp"),
        P("mp"),
        P("ctx", "mp"),
        P("ctx", None),
        P("ctx", None),
        P("mp", None, "ctx"),
        P("mp", None, "ctx"),
        P("mp", "ctx", None),
    )
    out_specs = (P("ctx", "mp"), P("ctx", "mp"), P("ctx", "mp"))
    return jax.shard_map(
        on_device, mesh=mesh, in_specs=in_specs, out_specs=out_specs, check_vma=False
    )
```

```python
import math

import jax
import jax.numpy as jnp
from jax import lax
from jax.experimental import pallas as pl
from jax.experimental.pallas import tpu as pltpu
from jax.sharding import PartitionSpec as P

HEAD_DIM = 128
HELD = 4
SEG = 128
CAP = 32
LOG2E = math.log2(math.e)
MESH = pl.DeviceIdType.MESH
F32 = jnp.float32
BF16 = jnp.bfloat16
HIGH = lax.Precision.HIGHEST


def dot(a, b, precision=None):
    return jnp.dot(a, b, preferred_element_type=F32, precision=precision)


def dot_nt(a, b, precision=None):
    return lax.dot_general(
        a, b, (((1,), (1,)), ((), ())), preferred_element_type=F32, precision=precision
    )


def iota(shape, dim):
    return lax.broadcasted_iota(jnp.int32, shape, dim)


def kernel(
    x_hbm, b_ref, c_ref, dt_ref, rate_ref, skip_ref, doc_ref, q_hbm, key_ref, val_ref, scale_ref,
    moe_ref, ids_ref, rw_ref, wg_ref, wu_ref, wd_ref,
    ssd_hbm, attn_hbm, moe_hbm,
    x_ref, q_ref, docr_ref, docc_ref, st_ref, ssd_out, attn_out, moe_out,
    wgu, wd, xs, pk, ptt, share, pl_land, l1, l2, qs, l3, l4, rx, fin, gu, hid,
    ka, va, sb, sl, en, er, t0s, ys, m_s, l_s, acc_s,
    w_sem, own_sem,
    xa_s, xa_r, sm_s, sm_r, bg_s, bg_r, bf_s, bf_r, cx_s, cx_r,
    cd_s, cd_r, ra_s, ra_r, rb_s, rb_r, xb_s, xb_r,
    ks_s, ks_r, out_sem, sa_s, sa_r, se_s, se_r,
):
    c = lax.axis_index("ctx")
    m = lax.axis_index("mp")
    z, y = c // 4, c % 4
    x, g = m // 2, m % 2
    sib = {"ctx": c, "mp": x * 2 + (1 - g)}

    def zy(zz, yy):
        return {"ctx": (zz % 4) * 4 + yy % 4, "mp": m}

    def xdev(xx):
        return {"ctx": c, "mp": (xx % 4) * 2 + g}

    def ctx(cc):
        return {"ctx": cc % 16, "mp": m}

    def remote(src, dst, s, r, dev):
        return pltpu.make_async_remote_copy(
            src_ref=src, dst_ref=dst, send_sem=s, recv_sem=r, device_id=dev, device_id_type=MESH
        )

    loads = [
        pltpu.make_async_copy(wg_ref.at[0], wgu.at[:, pl.ds(0, 384)], w_sem.at[0]),
        pltpu.make_async_copy(wu_ref.at[0], wgu.at[:, pl.ds(384, 384)], w_sem.at[1]),
        pltpu.make_async_copy(wd_ref.at[0], wd, w_sem.at[2]),
    ]
    heads_in = [
        pltpu.make_async_copy(key_ref, ka.at[z, y, pl.ds(0, 256)], own_sem.at[1]),
        pltpu.make_async_copy(val_ref, va.at[z, y], own_sem.at[5]),
        pltpu.make_async_copy(x_hbm, x_ref, own_sem.at[6]),
        pltpu.make_async_copy(q_hbm, q_ref, own_sem.at[7]),
    ]
    for load in heads_in + loads:
        load.start()

    bar = pltpu.get_barrier_semaphore()
    for k in range(1, 16):
        pl.semaphore_signal(bar, inc=1, device_id=ctx(c + k), device_id_type=MESH)
    for k in range(1, 4):
        pl.semaphore_signal(bar, inc=1, device_id=xdev(x + k), device_id_type=MESH)
    pl.semaphore_signal(bar, inc=1, device_id=sib, device_id_type=MESH)

    docs = doc_ref[...].astype(F32)
    docr_ref[...] = jnp.broadcast_to(docs, (8, 256))
    docc_ref[...] = jnp.broadcast_to(docs, (128, 256)).T
    ka[z, y, pl.ds(256, 16), :] = jnp.where(
        iota((16, 128), 0) == 0, docs[:, 0:128], docs[:, 128:256]
    ).astype(BF16)
    growth = jnp.log((c * 256 + 1 + iota((256, 128), 0)).astype(F32))
    lane = iota((256, 128), 1)
    slope = jnp.zeros((256, 128), F32)
    for h in range(8):
        slope = jnp.where(lane == h, scale_ref[h], slope)
    st_ref[...] = (1.0 + slope * growth) * (LOG2E / math.sqrt(HEAD_DIM))

    expert = iota((8, 256), 0)
    ids0, ids1 = ids_ref[0:1, :], ids_ref[1:2, :]
    named = ((ids0 == expert) | (ids1 == expert)).astype(F32)
    weight = jnp.where(ids0 == expert, rw_ref[0:1, :], 0.0) + jnp.where(
        ids1 == expert, rw_ref[1:2, :], 0.0
    )
    upto = (iota((256, 256), 0) <= iota((256, 256), 1)).astype(BF16)
    rank = dot(named.astype(BF16), upto).astype(jnp.int32) - 1
    slot = iota((CAP, 256), 0)
    for e in range(HELD):
        place = jnp.where((rank[e : e + 1, :] == slot) & (named[e : e + 1, :] > 0.0), 1.0, 0.0)
        pk[e] = dot(place.astype(BF16), moe_ref[...]).astype(BF16)
        share[pl.ds(e * CAP, CAP), :] = jnp.broadcast_to(
            jnp.sum(place * weight[e : e + 1, :], axis=1, keepdims=True), (CAP, 128)
        )
        ptt[pl.ds(e * CAP, CAP), :] = place

    pl.semaphore_wait(bar, 19)

    xa = []
    for k in range(1, 4):
        cp = remote(
            pk.at[(x + k) % 4], xs.at[g, x, z, y], xa_s.at[k - 1], xa_r.at[k - 1], xdev(x + k)
        )
        cp.start()
        xa.append(cp)
    own = pltpu.make_async_copy(pk.at[x], xs.at[g, x, z, y], own_sem.at[0])
    own.start()
    big = (z, y)
    small = (y, z)

    def big_dev(h, d):
        return zy(z + d, y) if h == 0 else zy(z, y + d)

    def small_dev(h, d):
        return zy(z, y + d) if h == 0 else zy(z + d, y)

    key_rows = ((0, 144), (144, 128)), ((0, 128), (128, 128))

    def kcp(h, n, i, k, j, dev):
        arr = (ka, va)[h]
        rows = pl.ds(*key_rows[h][j]) if j is not None else slice(None)
        if k is None:
            v = arr.at[i % 4, :, rows] if h == 0 else arr.at[:, i % 4, rows]
        else:
            v = arr.at[i % 4, k % 4, rows] if h == 0 else arr.at[k % 4, i % 4, rows]
        return remote(v, v, ks_s.at[h, n], ks_r.at[h, n], dev)

    def k_small(h, d):
        return kcp(h, 0 if d == 1 else 1, big[h], small[h], None, small_dev(h, d))

    def k_small_fwd(h, d):
        n, j = (2, 0) if d == 1 else (3, 1)
        return kcp(h, n, big[h], small[h] - d + 4, j, small_dev(h, d))

    def k_big(h, d):
        return kcp(h, 4 if d == 1 else 5, big[h], None, None, big_dev(h, d))

    def k_big_fwd(h, d):
        n, j = (6, 0) if d == 1 else (7, 1)
        return kcp(h, n, big[h] - d + 4, None, j, big_dev(h, d))

    sends = []
    k_sends = []

    def go(cp, kept=None):
        cp.start()
        (sends if kept is None else kept).append(cp)

    heads_in[0].wait()
    heads_in[1].wait()
    for h in range(2):
        for d in (1, -1):
            go(k_small(h, d), k_sends)
    heads_in[2].wait()

    low = iota((SEG, SEG), 0) >= iota((SEG, SEG), 1)
    tri = low.astype(F32)
    cum_r, cum_c, inner, linked, bt = [], [], [], [], []
    rate = jnp.zeros((8, 1), F32)
    for h in range(8):
        rate = jnp.where(iota((8, 1), 0) == h, rate_ref[h], rate)
    for k in range(2):
        rows = slice(k * SEG, (k + 1) * SEG)
        ld = -(dt_ref[:, rows] * rate)
        cum_r.append(dot_nt(ld, tri, HIGH))
        cum_c.append(dot_nt(tri, ld, HIGH))
        inner.append(dot_nt(c_ref[rows, :], b_ref[rows, :]))
        linked.append((docc_ref[rows, :] == docr_ref[0:1, rows]) & low)
        bt.append(b_ref[rows, :].astype(F32).T)
    first = [docr_ref[:, k * SEG : k * SEG + 1] for k in range(2)]
    last = [docr_ref[:, k * SEG + SEG - 1 : (k + 1) * SEG] for k in range(2)]
    dec = [
        jnp.exp(cum_r[k][:, SEG - 1 : SEG]) * (first[k] == last[k]).astype(F32) for k in range(2)
    ]
    tail = [
        jnp.where(
            docr_ref[:, k * SEG : (k + 1) * SEG] == last[k],
            jnp.exp(cum_r[k][:, SEG - 1 : SEG] - cum_r[k]),
            0.0,
        )
        for k in range(2)
    ]
    lift = [
        jnp.exp(cum_c[k])
        * (docc_ref[k * SEG : (k + 1) * SEG, 0:8] == first[k][0:1, :]).astype(F32)
        for k in range(2)
    ]
    joined = (last[0] == first[1]).astype(F32)
    whole = dec[1] * joined * dec[0]

    def head_states(h):
        cols = slice(h * 256, (h + 1) * 256)
        locs = []
        for k in range(2):
            rows = slice(k * SEG, (k + 1) * SEG)
            xb = x_ref[rows, cols]
            locs.append(dot((bt[k] * tail[k][h : h + 1, :]).astype(BF16), xb))
        t0s[h] = locs[0]
        total = locs[1] + (dec[1] * joined)[h : h + 1, :] * locs[0]
        row = iota((16, 128), 0)
        w = jnp.broadcast_to(whole[h : h + 1, :], (16, 128))
        w_hi = w.astype(BF16).astype(F32)
        info = jnp.where(
            row == 0,
            w_hi,
            jnp.where(
                row == 1,
                w - w_hi,
                jnp.where(row == 2, first[0][0:1, :], last[1][0:1, :]),
            ),
        ).astype(BF16)
        for half in range(2):
            sb[2 * h + half, pl.ds(0, 128), :] = total[:, half * 128 : half * 128 + 128].astype(
                BF16
            )
            sb[2 * h + half, pl.ds(128, 16), :] = info

    def head_inside(h):
        cols = slice(h * 256, (h + 1) * 256)
        for k in range(2):
            rows = slice(k * SEG, (k + 1) * SEG)
            xb = x_ref[rows, cols]
            gap = cum_c[k][:, h : h + 1] - cum_r[k][h : h + 1, :]
            w = jnp.where(linked[k], inner[k] * jnp.exp(jnp.where(linked[k], gap, 0.0)), 0.0)
            ys[rows, cols] = dot(w.astype(BF16), xb) + skip_ref[h] * xb.astype(F32)

    for h in range(8):
        head_states(h)

    def state_out(k):
        return remote(sb.at[(c + k) % 16], sl.at[c], sa_s.at[k], sa_r.at[k], ctx(c + k))

    states = []
    for k in range(1, 16):
        go(state_out(k), states)
    mine = pltpu.make_async_copy(sb.at[c], sl.at[c], own_sem.at[2])
    mine.start()

    own.wait()
    for cp in xa:
        cp.wait()

    def xv(h, j, i, k):
        cols = pl.ds(2 * h, 2) if j is None else 2 * h + j
        return xs.at[g, cols, i % 4, k % 4] if h == 0 else xs.at[g, cols, k % 4, i % 4]

    order = (0, -1, 1, 2)

    def cp_small(h, d):
        v = xv(h, None, big[h], small[h])
        n = 0 if d == 1 else 1
        return remote(v, v, sm_s.at[h, n], sm_r.at[h, n], small_dev(h, d))

    def cp_small_fwd(h, d):
        n, j = (2, 0) if d == 1 else (3, 1)
        v = xv(h, j, big[h], small[h] - d + 4)
        return remote(v, v, sm_s.at[h, n], sm_r.at[h, n], small_dev(h, d))

    def cp_big(h, d, r):
        n = 0 if d == 1 else 1
        v = xv(h, None, big[h], small[h] + order[r] + 4)
        return remote(v, v, bg_s.at[h, n, r], bg_r.at[h, n, r], big_dev(h, d))

    def cp_big_fwd(h, d, r):
        n = 0 if d == 1 else 1
        v = xv(h, n, big[h] - d + 4, small[h] + order[r] + 4)
        return remote(v, v, bf_s.at[h, n, r], bf_r.at[h, n, r], big_dev(h, d))

    def cp_cross(h, d):
        i = (big[h] + d + 4) % 4
        cols = pl.ds(2 * h, 2)
        v = xs.at[g, cols, i] if h == 0 else xs.at[g, cols, :, i]
        return remote(v, v, cx_s.at[h, d % 4], cx_r.at[h, d % 4], sib)

    m_s[...] = jnp.full_like(m_s, -1e30)
    l_s[...] = jnp.zeros_like(l_s)
    acc_s[...] = jnp.zeros_like(acc_s)

    def absorb(k, diagonal):
        there = c - k
        keys = ka[there // 4, there % 4, pl.ds(0, 256), :]
        vals = va[there // 4, there % 4]
        docs = ka[there // 4, there % 4, pl.ds(256, 16), :].astype(F32)
        doc_row = jnp.concatenate([docs[0:1, :], docs[1:2, :]], axis=1)
        docc = docc_ref[...]
        allowed = jnp.concatenate([docc, docc], axis=1) == doc_row
        if diagonal:
            allowed = allowed & (iota((256, 256), 0) >= iota((256, 256), 1))
        bias = jnp.where(allowed, 0.0, -1e30)
        for h in range(8):
            s = dot_nt(q_ref[:, h * 128 : h * 128 + 128], keys) + bias
            st = st_ref[:, h : h + 1]
            old = m_s[h][:, 0:1]
            new = jnp.maximum(old, jnp.max(s, axis=1, keepdims=True))
            p = jnp.exp2((s - new) * st)
            fade = jnp.exp2((old - new) * st)
            l_s[h] = l_s[h] * fade + jnp.sum(p, axis=1, keepdims=True)
            acc_s[h] = acc_s[h] * fade + dot(p.astype(BF16), vals)
            m_s[h] = jnp.broadcast_to(new, (256, 128))

    def absorb_range(lo, hi):
        def body(k, carry):
            absorb(k, False)
            return carry

        lax.fori_loop(lo, jnp.maximum(jnp.minimum(c + 1, hi), lo), body, 0)

    for h in range(2):
        for d in (1, -1):
            go(cp_small(h, d))
    for h in range(2):
        for d in (1, -1):
            go(cp_big(h, d, 0))

    head_inside(0)
    head_inside(1)

    for d, r in ((1, 1), (-1, 2)):
        for h in range(2):
            cp_small(h, d).wait_recv()
            go(cp_small_fwd(h, d))
            for e in (1, -1):
                go(cp_big(h, e, r))
    for h in range(2):
        for d in (1, -1):
            k_small(h, d).wait_recv()
            go(k_small_fwd(h, d), k_sends)
    heads_in[3].wait()
    absorb(0, True)
    for h in range(2):
        for d in (1, -1):
            cp_small_fwd(h, d).wait_recv()
        for e in (1, -1):
            go(cp_big(h, e, 3))
        go(cp_cross(h, 0))

    def pass_on(r):
        for h in range(2):
            for d in (1, -1):
                cp_big(h, d, r).wait_recv()
                go(cp_big_fwd(h, d, r))

    head_inside(2)
    pass_on(0)
    for h in range(2):
        for d in (1, -1):
            k_small_fwd(h, d).wait_recv()
    head_inside(3)
    head_inside(4)
    pass_on(1)
    pass_on(2)
    head_inside(5)
    head_inside(6)
    head_inside(7)
    pass_on(3)
    for h in range(2):
        go(cp_cross(h, -1))
        go(cp_cross(h, 1))
    for h in range(2):
        for d in (1, -1):
            go(k_big(h, d), k_sends)
    mine.wait()

    def scan(i, carry):
        state, before = carry

        @pl.when(i != c)
        def _():
            k = (c - i + 16) % 16
            remote(
                sb.at[c], sl.at[i], sa_s.at[k], sa_r.at[k], ctx(c + 1)
            ).wait_recv()

        info = sl[i, pl.ds(128, 16), :].astype(F32)
        entering = jnp.where(before == info[2:3, :], state, 0.0)
        en[i] = entering.astype(BF16)
        state = (info[0:1, :] + info[1:2, :]) * entering + sl[i, pl.ds(0, 128), :].astype(F32)
        return state, info[3:4, :]

    lax.fori_loop(
        0, 16, scan, (jnp.zeros((128, 128), F32), jnp.full((1, 128), -1.0, F32))
    )

    def state_back(k):
        return remote(en.at[(c + k) % 16], er.at[c], se_s.at[k], se_r.at[k], ctx(c + k))

    backs = []
    for k in range(1, 16):
        go(state_back(k), backs)
    mine_back = pltpu.make_async_copy(en.at[c], er.at[c], own_sem.at[3])
    mine_back.start()

    for h in range(2):
        for r in range(4):
            for d in (1, -1):
                cp_big_fwd(h, d, r).wait_recv()
        go(cp_cross(h, 2))
    for cp in sends:
        cp.wait_send()

    def cross_in(h, d):
        i = (big[h] + d + 4) % 4
        cols = pl.ds(2 * h, 2)
        v = xs.at[1 - g, cols, i] if h == 0 else xs.at[1 - g, cols, :, i]
        return remote(v, v, cx_s.at[h, d % 4], cx_r.at[h, d % 4], sib)

    for h in range(2):
        for d in (0, -1, 1, 2):
            cross_in(h, d).wait_recv()
    for load in loads:
        load.wait()

    gu[...] = jnp.zeros_like(gu)

    def gate_up(i, carry):
        gg, xx = i // 4, i % 4
        block = pl.multiple_of((xx * 2 + gg) * 1024, 1024)
        gu[...] += dot(xs[gg, xx].reshape(512, 1024), wgu[pl.ds(block, 1024), :])
        return carry

    lax.fori_loop(0, 4, gate_up, 0)
    for h in range(2):
        for d in (1, -1):
            k_big(h, d).wait_recv()
            go(k_big_fwd(h, d), k_sends)
    lax.fori_loop(4, 8, gate_up, 0)
    gate, up = gu[:, 0:384], gu[:, 384:768]
    hid[...] = (gate / (1.0 + jnp.exp(-gate)) * up).astype(BF16)

    ps, pa = xs.at[0], xs.at[1]

    def cp_down(xx):
        return remote(ps.at[xx], pl_land.at[xx], cd_s.at[xx], cd_r.at[xx], sib)

    for xx in (0, 2, 1, 3):

        def down_sib(n, carry):
            off = pl.multiple_of(n * 512, 512)
            col = pl.multiple_of((xx * 2 + 1 - g) * 1024 + n * 512, 512)
            r = dot(hid[...], wd[:, pl.ds(col, 512)])
            ps[xx, :, :, :, pl.ds(off, 512)] = r.astype(BF16).reshape(4, 4, CAP, 512)
            return carry

        lax.fori_loop(0, 2, down_sib, 0)
        cp_down(xx).start()

    def pv(h, j, i):
        return pa.at[2 * h + j, i % 4] if h == 0 else pa.at[2 * h + j, :, i % 4]

    def ra_first(h, j):
        d = 1 if j == 0 else -1
        return remote(
            pv(h, j, big[h] + 2), l1.at[h, j], ra_s.at[h, j], ra_r.at[h, j], big_dev(h, d)
        )

    def ra_block(h, j, d):
        n = 0 if d == 1 else 1
        return remote(
            pv(h, j, big[h] + d + 4),
            l2.at[h, n, j],
            ra_s.at[h, 2 + 2 * n + j],
            ra_r.at[h, 2 + 2 * n + j],
            big_dev(h, d),
        )

    for xx in (0, 2, 1, 3):
        cp_down(xx).wait_recv()

        def down_own(n, carry):
            off = pl.multiple_of(n * 512, 512)
            col = pl.multiple_of((xx * 2 + g) * 1024 + n * 512, 512)
            r = dot(hid[...], wd[:, pl.ds(col, 512)])
            r = r.reshape(4, 4, CAP, 512) + pl_land[xx, :, :, :, pl.ds(off, 512)].astype(F32)
            pa[xx, :, :, :, pl.ds(off, 512)] = r.astype(BF16)
            return carry

        lax.fori_loop(0, 2, down_own, 0)
        h, j = xx // 2, xx % 2
        ra_first(h, j).start()
        ra_block(h, j, -1 if j == 0 else 1).start()


    for h in range(2):
        for d in (1, -1):
            k_big_fwd(h, d).wait_recv()
    absorb_range(1, 3)

    for h in range(2):
        ra_first(h, 0).wait_recv()
        v = pv(h, 0, big[h] + 1)
        v[...] = (v[...].astype(F32) + l1[h, 0].astype(F32)).astype(BF16)
        ra_block(h, 0, 1).start()
        ra_first(h, 1).wait_recv()
        v = pv(h, 1, big[h] + 3)
        v[...] = (v[...].astype(F32) + l1[h, 1].astype(F32)).astype(BF16)
        ra_block(h, 1, -1).start()

    absorb_range(3, 7)

    def rb_first(h, j):
        d = 1 if j == 0 else -1
        return remote(
            qs.at[h, j, (small[h] + 2) % 4],
            l3.at[h, j],
            rb_s.at[h, j],
            rb_r.at[h, j],
            small_dev(h, d),
        )

    def rb_block(h, j, d):
        n = 0 if d == 1 else 1
        return remote(
            qs.at[h, j, (small[h] + d + 4) % 4],
            l4.at[h, n, j],
            rb_s.at[h, 2 + 2 * n + j],
            rb_r.at[h, 2 + 2 * n + j],
            small_dev(h, d),
        )

    for h in range(2):
        for j in range(2):
            for d in (1, -1):
                ra_block(h, j, d).wait_recv()
            qs[h, j] = (
                pv(h, j, big[h])[...].astype(F32)
                + l2[h, 0, j].astype(F32)
                + l2[h, 1, j].astype(F32)
            ).astype(BF16)
            rb_first(h, j).start()
            rb_block(h, j, -1 if j == 0 else 1).start()

    absorb_range(7, 8)

    for h in range(2):
        for j, d in ((0, 1), (1, -1)):
            rb_first(h, j).wait_recv()
            v = qs.at[h, j, (small[h] + d + 4) % 4]
            v[...] = (v[...].astype(F32) + l3[h, j].astype(F32)).astype(BF16)
            rb_block(h, j, d).start()

    absorb_range(8, 9)

    share_x = share[pl.ds(pl.multiple_of(x * CAP, CAP), CAP), 0:1]

    def x_back(k):
        return remote(
            rx.at[(x + k) % 4], fin.at[x], xb_s.at[k - 1], xb_r.at[k - 1], xdev(x + k)
        )

    for h in range(2):
        for j in range(2):
            for d in (1, -1):
                rb_block(h, j, d).wait_recv()
            total = (
                qs[h, j, small[h]].astype(F32)
                + l4[h, 0, j].astype(F32)
                + l4[h, 1, j].astype(F32)
            )
            rx[2 * h + j] = (total * share_x).astype(BF16)
    for k in range(1, 4):
        x_back(k).start()
    own_back = pltpu.make_async_copy(rx.at[x], fin.at[x], own_sem.at[4])
    own_back.start()

    for h in range(8):
        attn_out[:, h * 128 : h * 128 + 128] = (acc_s[h] / l_s[h]).astype(BF16)
    attn_done = pltpu.make_async_copy(attn_out, attn_hbm, out_sem.at[0])
    attn_done.start()

    mine_back.wait()
    for cp in backs:
        cp.wait()
    for h in range(8):
        cols = slice(h * 256, (h + 1) * 256)
        e0 = jnp.concatenate([er[2 * h], er[2 * h + 1]], axis=1)
        e1 = (
            joined[h : h + 1, :] * (dec[0][h : h + 1, :] * e0.astype(F32) + t0s[h])
        ).astype(BF16)
        for k, e in ((0, e0), (1, e1)):
            rows = slice(k * SEG, (k + 1) * SEG)
            carried = dot(c_ref[rows, :], e)
            ssd_out[rows, cols] = (ys[rows, cols] + carried * lift[k][:, h : h + 1]).astype(BF16)

    ssd_done = pltpu.make_async_copy(ssd_out, ssd_hbm, out_sem.at[1])
    ssd_done.start()

    own_back.wait()
    for k in range(1, 4):
        x_back(k).wait()
    moe_out[...] = dot(ptt[...].T.astype(BF16), fin[...].reshape(128, 1024)).astype(BF16)

    moe_done = pltpu.make_async_copy(moe_out, moe_hbm, out_sem.at[2])
    moe_done.start()

    for cp in k_sends:
        cp.wait_send()
    for cp in states:
        cp.wait_send()
    for xx in range(4):
        cp_down(xx).wait_send()
    for h in range(2):
        for j in range(2):
            ra_first(h, j).wait_send()
            rb_first(h, j).wait_send()
            for d in (1, -1):
                ra_block(h, j, d).wait_send()
                rb_block(h, j, d).wait_send()
    attn_done.wait()
    ssd_done.wait()
    moe_done.wait()


def settle(*refs):
    sources, results, held, sems = refs[0:3], refs[3:6], refs[6:9], refs[9]
    parts = []
    for i in range(3):
        for p in range(2):
            rows = pl.ds(p * 128, 128)
            into = pltpu.make_async_copy(
                sources[i].at[rows], held[i].at[rows], sems.at[0, i, p]
            )
            back = pltpu.make_async_copy(
                held[i].at[rows], results[i].at[rows], sems.at[1, i, p]
            )
            into.start()
            parts.append((into, back))
    for into, back in parts:
        into.wait()
        back.start()
    for into, back in parts:
        back.wait()


def on_device(
    ssd_x, ssd_b, ssd_c, dt_steps, decay_rate, skip_gain, doc_ids,
    queries, key_rows, values, log_scale,
    moe_in, expert_ids, route_weights, w_gate, w_up, w_down,
):
    positions = ssd_x.shape[0]
    vmem = pl.BlockSpec(memory_space=pltpu.VMEM)
    smem = pl.BlockSpec(memory_space=pltpu.SMEM)
    anyw = pl.BlockSpec(memory_space=pl.ANY)
    dma = pltpu.SemaphoreType.DMA
    shapes = (
        jax.ShapeDtypeStruct((positions, 2048), BF16),
        jax.ShapeDtypeStruct((positions, 1024), BF16),
        jax.ShapeDtypeStruct((positions, 1024), BF16),
    )
    made = pl.pallas_call(
        kernel,
        out_shape=shapes,
        in_specs=[anyw, vmem, vmem, vmem, smem, smem, vmem, anyw, anyw, anyw, smem]
        + [vmem] * 3
        + [anyw] * 3,
        out_specs=(anyw, anyw, anyw),
        scratch_shapes=[
            pltpu.VMEM((256, 2048), BF16),
            pltpu.VMEM((256, 1024), BF16),
            pltpu.VMEM((8, 256), F32),
            pltpu.VMEM((256, 128), F32),
            pltpu.VMEM((256, 128), F32),
            pltpu.VMEM((256, 2048), BF16),
            pltpu.VMEM((256, 1024), BF16),
            pltpu.VMEM((256, 1024), BF16),
            pltpu.VMEM((8192, 768), BF16),
            pltpu.VMEM((384, 8192), BF16),
            pltpu.VMEM((2, 4, 4, 4, CAP, 1024), BF16),
            pltpu.VMEM((4, CAP, 1024), BF16),
            pltpu.VMEM((128, 256), F32),
            pltpu.VMEM((128, 128), F32),
            pltpu.VMEM((4, 4, 4, CAP, 1024), BF16),
            pltpu.VMEM((2, 2, 4, CAP, 1024), BF16),
            pltpu.VMEM((2, 2, 2, 4, CAP, 1024), BF16),
            pltpu.VMEM((2, 2, 4, CAP, 1024), BF16),
            pltpu.VMEM((2, 2, CAP, 1024), BF16),
            pltpu.VMEM((2, 2, 2, CAP, 1024), BF16),
            pltpu.VMEM((4, CAP, 1024), BF16),
            pltpu.VMEM((4, CAP, 1024), BF16),
            pltpu.VMEM((512, 768), F32),
            pltpu.VMEM((512, 384), BF16),
            pltpu.VMEM((4, 4, 272, 128), BF16),
            pltpu.VMEM((4, 4, 256, 128), BF16),
            pltpu.VMEM((16, 144, 128), BF16),
            pltpu.VMEM((16, 144, 128), BF16),
            pltpu.VMEM((16, 128, 128), BF16),
            pltpu.VMEM((16, 128, 128), BF16),
            pltpu.VMEM((8, 128, 256), F32),
            pltpu.VMEM((256, 2048), F32),
            pltpu.VMEM((8, 256, 128), F32),
            pltpu.VMEM((8, 256, 128), F32),
            pltpu.VMEM((8, 256, 128), F32),
            dma((3,)),
            dma((8,)),
            dma((3,)), dma((3,)),
            dma((2, 4)), dma((2, 4)),
            dma((2, 2, 4)), dma((2, 2, 4)),
            dma((2, 2, 4)), dma((2, 2, 4)),
            dma((2, 4)), dma((2, 4)),
            dma((4,)), dma((4,)),
            dma((2, 6)), dma((2, 6)),
            dma((2, 6)), dma((2, 6)),
            dma((3,)), dma((3,)),
            dma((2, 8)), dma((2, 8)),
            dma((3,)),
            dma((16,)), dma((16,)),
            dma((16,)), dma((16,)),
        ],
        compiler_params=pltpu.CompilerParams(
            collective_id=0, has_side_effects=True, vmem_limit_bytes=60 * 2**20
        ),
        name="layer_pair",
    )(
        ssd_x, ssd_b, ssd_c, dt_steps, decay_rate, skip_gain, doc_ids[None, :],
        queries, key_rows, values, log_scale,
        moe_in, expert_ids.T, route_weights.T, w_gate, w_up, w_down,
    )
    return pl.pallas_call(
        settle,
        out_shape=shapes,
        in_specs=[anyw] * 3,
        out_specs=(anyw, anyw, anyw),
        scratch_shapes=[
            pltpu.VMEM((256, 2048), BF16),
            pltpu.VMEM((256, 1024), BF16),
            pltpu.VMEM((256, 1024), BF16),
            dma((2, 3, 2)),
        ],
        compiler_params=pltpu.CompilerParams(vmem_limit_bytes=60 * 2**20),
        name="settle",
    )(*made)


def solution(mesh):
    in_specs = (
        P("ctx", "mp"),
        P("ctx", None),
        P("ctx", None),
        P("mp", "ctx"),
        P("mp"),
        P("mp"),
        P("ctx"),
        P("ctx", "mp"),
        P("ctx", "mp"),
        P("ctx", "mp"),
        P("mp"),
        P("ctx", "mp"),
        P("ctx", None),
        P("ctx", None),
        P("mp", None, "ctx"),
        P("mp", None, "ctx"),
        P("mp", "ctx", None),
    )
    out_specs = (P("ctx", "mp"), P("ctx", "mp"), P("ctx", "mp"))
    return jax.shard_map(
        on_device, mesh=mesh, in_specs=in_specs, out_specs=out_specs, check_vma=False
    )
```

```python
import math

import jax
import jax.numpy as jnp
from jax import lax
from jax.experimental import pallas as pl
from jax.experimental.pallas import tpu as pltpu
from jax.sharding import PartitionSpec as P

HEAD_DIM = 128
HELD = 4
SEG = 128
CAP = 32
LOG2E = math.log2(math.e)
MESH = pl.DeviceIdType.MESH
F32 = jnp.float32
BF16 = jnp.bfloat16
HIGH = lax.Precision.HIGHEST


def dot(a, b, precision=None):
    return jnp.dot(a, b, preferred_element_type=F32, precision=precision)


def dot_nt(a, b, precision=None):
    return lax.dot_general(
        a, b, (((1,), (1,)), ((), ())), preferred_element_type=F32, precision=precision
    )


def iota(shape, dim):
    return lax.broadcasted_iota(jnp.int32, shape, dim)


def kernel(
    x_hbm, b_ref, c_ref, dt_ref, rate_ref, skip_ref, doc_ref, q_hbm, key_ref, val_ref, scale_ref,
    moe_ref, ids_ref, rw_ref, wg_ref, wu_ref, wd_ref,
    ssd_hbm, attn_hbm, moe_hbm,
    x_ref, q_ref, docr_ref, docc_ref, st_ref, ssd_out, attn_out, moe_out,
    wgu, wd, xs, pk, ptt, share, pl_land, l1, l2, qs, l3, l4, rx, fin, gu, hid,
    ka, va, sb, sl, en, er, t0s, ys, m_s, l_s, acc_s,
    w_sem, own_sem,
    xa_s, xa_r, sm_s, sm_r, bg_s, bg_r, bf_s, bf_r, cx_s, cx_r,
    cd_s, cd_r, ra_s, ra_r, rb_s, rb_r, xb_s, xb_r,
    ks_s, ks_r, out_sem, sa_s, sa_r, se_s, se_r,
):
    c = lax.axis_index("ctx")
    m = lax.axis_index("mp")
    z, y = c // 4, c % 4
    x, g = m // 2, m % 2
    sib = {"ctx": c, "mp": x * 2 + (1 - g)}

    def zy(zz, yy):
        return {"ctx": (zz % 4) * 4 + yy % 4, "mp": m}

    def xdev(xx):
        return {"ctx": c, "mp": (xx % 4) * 2 + g}

    def ctx(cc):
        return {"ctx": cc % 16, "mp": m}

    def remote(src, dst, s, r, dev):
        return pltpu.make_async_remote_copy(
            src_ref=src, dst_ref=dst, send_sem=s, recv_sem=r, device_id=dev, device_id_type=MESH
        )

    loads = [
        pltpu.make_async_copy(wg_ref.at[0], wgu.at[:, pl.ds(0, 384)], w_sem.at[0]),
        pltpu.make_async_copy(wu_ref.at[0], wgu.at[:, pl.ds(384, 384)], w_sem.at[1]),
        pltpu.make_async_copy(wd_ref.at[0], wd, w_sem.at[2]),
    ]
    heads_in = [
        pltpu.make_async_copy(key_ref, ka.at[z, y, pl.ds(0, 256)], own_sem.at[1]),
        pltpu.make_async_copy(val_ref, va.at[z, y], own_sem.at[5]),
        pltpu.make_async_copy(x_hbm, x_ref, own_sem.at[6]),
        pltpu.make_async_copy(q_hbm, q_ref, own_sem.at[7]),
    ]
    for load in heads_in + loads:
        load.start()

    bar = pltpu.get_barrier_semaphore()
    for k in range(1, 16):
        pl.semaphore_signal(bar, inc=1, device_id=ctx(c + k), device_id_type=MESH)
    for k in range(1, 4):
        pl.semaphore_signal(bar, inc=1, device_id=xdev(x + k), device_id_type=MESH)
    pl.semaphore_signal(bar, inc=1, device_id=sib, device_id_type=MESH)

    docs = doc_ref[...].astype(F32)
    docr_ref[...] = jnp.broadcast_to(docs, (8, 256))
    docc_ref[...] = jnp.broadcast_to(docs, (128, 256)).T
    ka[z, y, pl.ds(256, 16), :] = jnp.where(
        iota((16, 128), 0) == 0, docs[:, 0:128], docs[:, 128:256]
    ).astype(BF16)
    growth = jnp.log((c * 256 + 1 + iota((8, 256), 1)).astype(F32))
    slope = jnp.zeros((8, 256), F32)
    for h in range(8):
        slope = jnp.where(iota((8, 256), 0) == h, scale_ref[h], slope)
    st_ref[...] = (1.0 + slope * growth) * (LOG2E / math.sqrt(HEAD_DIM))

    expert = iota((8, 256), 0)
    ids0, ids1 = ids_ref[0:1, :], ids_ref[1:2, :]
    named = ((ids0 == expert) | (ids1 == expert)).astype(F32)
    weight = jnp.where(ids0 == expert, rw_ref[0:1, :], 0.0) + jnp.where(
        ids1 == expert, rw_ref[1:2, :], 0.0
    )
    upto = (iota((256, 256), 0) <= iota((256, 256), 1)).astype(BF16)
    rank = dot(named.astype(BF16), upto).astype(jnp.int32) - 1
    slot = iota((CAP, 256), 0)
    for e in range(HELD):
        place = jnp.where((rank[e : e + 1, :] == slot) & (named[e : e + 1, :] > 0.0), 1.0, 0.0)
        pk[e] = dot(place.astype(BF16), moe_ref[...]).astype(BF16)
        share[pl.ds(e * CAP, CAP), :] = jnp.broadcast_to(
            jnp.sum(place * weight[e : e + 1, :], axis=1, keepdims=True), (CAP, 128)
        )
        ptt[pl.ds(e * CAP, CAP), :] = place

    pl.semaphore_wait(bar, 19)

    xa = []
    for k in range(1, 4):
        cp = remote(
            pk.at[(x + k) % 4], xs.at[g, x, z, y], xa_s.at[k - 1], xa_r.at[k - 1], xdev(x + k)
        )
        cp.start()
        xa.append(cp)
    own = pltpu.make_async_copy(pk.at[x], xs.at[g, x, z, y], own_sem.at[0])
    own.start()
    big = (z, y)
    small = (y, z)

    def big_dev(h, d):
        return zy(z + d, y) if h == 0 else zy(z, y + d)

    def small_dev(h, d):
        return zy(z, y + d) if h == 0 else zy(z + d, y)

    key_rows = ((0, 144), (144, 128)), ((0, 128), (128, 128))

    def kcp(h, n, i, k, j, dev):
        arr = (ka, va)[h]
        rows = pl.ds(*key_rows[h][j]) if j is not None else slice(None)
        if k is None:
            v = arr.at[i % 4, :, rows] if h == 0 else arr.at[:, i % 4, rows]
        else:
            v = arr.at[i % 4, k % 4, rows] if h == 0 else arr.at[k % 4, i % 4, rows]
        return remote(v, v, ks_s.at[h, n], ks_r.at[h, n], dev)

    def k_small(h, d):
        return kcp(h, 0 if d == 1 else 1, big[h], small[h], None, small_dev(h, d))

    def k_small_fwd(h, d):
        n, j = (2, 0) if d == 1 else (3, 1)
        return kcp(h, n, big[h], small[h] - d + 4, j, small_dev(h, d))

    def k_big(h, d):
        return kcp(h, 4 if d == 1 else 5, big[h], None, None, big_dev(h, d))

    def k_big_fwd(h, d):
        n, j = (6, 0) if d == 1 else (7, 1)
        return kcp(h, n, big[h] - d + 4, None, j, big_dev(h, d))

    sends = []
    k_sends = []

    def go(cp, kept=None):
        cp.start()
        (sends if kept is None else kept).append(cp)

    heads_in[0].wait()
    heads_in[1].wait()
    for h in range(2):
        for d in (1, -1):
            go(k_small(h, d), k_sends)
    heads_in[2].wait()

    low = iota((SEG, SEG), 0) >= iota((SEG, SEG), 1)
    tri = low.astype(F32)
    cum_r, cum_c, inner, linked, bt = [], [], [], [], []
    rate = jnp.zeros((8, 1), F32)
    for h in range(8):
        rate = jnp.where(iota((8, 1), 0) == h, rate_ref[h], rate)
    for k in range(2):
        rows = slice(k * SEG, (k + 1) * SEG)
        ld = -(dt_ref[:, rows] * rate)
        cum_r.append(dot_nt(ld, tri, HIGH))
        cum_c.append(dot_nt(tri, ld, HIGH))
        inner.append(dot_nt(c_ref[rows, :], b_ref[rows, :]))
        linked.append((docc_ref[rows, :] == docr_ref[0:1, rows]) & low)
        bt.append(b_ref[rows, :].astype(F32).T)
    first = [docr_ref[:, k * SEG : k * SEG + 1] for k in range(2)]
    last = [docr_ref[:, k * SEG + SEG - 1 : (k + 1) * SEG] for k in range(2)]
    dec = [
        jnp.exp(cum_r[k][:, SEG - 1 : SEG]) * (first[k] == last[k]).astype(F32) for k in range(2)
    ]
    tail = [
        jnp.where(
            docr_ref[:, k * SEG : (k + 1) * SEG] == last[k],
            jnp.exp(cum_r[k][:, SEG - 1 : SEG] - cum_r[k]),
            0.0,
        )
        for k in range(2)
    ]
    lift = [
        jnp.exp(cum_c[k])
        * (docc_ref[k * SEG : (k + 1) * SEG, 0:8] == first[k][0:1, :]).astype(F32)
        for k in range(2)
    ]
    joined = (last[0] == first[1]).astype(F32)
    whole = dec[1] * joined * dec[0]

    def head_states(h):
        cols = slice(h * 256, (h + 1) * 256)
        locs = []
        for k in range(2):
            rows = slice(k * SEG, (k + 1) * SEG)
            xb = x_ref[rows, cols]
            locs.append(dot((bt[k] * tail[k][h : h + 1, :]).astype(BF16), xb))
        t0s[h] = locs[0]
        total = locs[1] + (dec[1] * joined)[h : h + 1, :] * locs[0]
        row = iota((16, 128), 0)
        w = jnp.broadcast_to(whole[h : h + 1, :], (16, 128))
        w_hi = w.astype(BF16).astype(F32)
        info = jnp.where(
            row == 0,
            w_hi,
            jnp.where(
                row == 1,
                w - w_hi,
                jnp.where(row == 2, first[0][0:1, :], last[1][0:1, :]),
            ),
        ).astype(BF16)
        for half in range(2):
            sb[2 * h + half, pl.ds(0, 128), :] = total[:, half * 128 : half * 128 + 128].astype(
                BF16
            )
            sb[2 * h + half, pl.ds(128, 16), :] = info

    def head_inside(h):
        cols = slice(h * 256, (h + 1) * 256)
        for k in range(2):
            rows = slice(k * SEG, (k + 1) * SEG)
            xb = x_ref[rows, cols]
            gap = cum_c[k][:, h : h + 1] - cum_r[k][h : h + 1, :]
            w = jnp.where(linked[k], inner[k] * jnp.exp(jnp.where(linked[k], gap, 0.0)), 0.0)
            ys[rows, cols] = dot(w.astype(BF16), xb) + skip_ref[h] * xb.astype(F32)

    for h in range(8):
        head_states(h)

    def state_out(k):
        return remote(sb.at[(c + k) % 16], sl.at[c], sa_s.at[k], sa_r.at[k], ctx(c + k))

    states = []
    for k in range(1, 16):
        go(state_out(k), states)
    mine = pltpu.make_async_copy(sb.at[c], sl.at[c], own_sem.at[2])
    mine.start()

    own.wait()
    for cp in xa:
        cp.wait()

    def xv(h, j, i, k):
        cols = pl.ds(2 * h, 2) if j is None else 2 * h + j
        return xs.at[g, cols, i % 4, k % 4] if h == 0 else xs.at[g, cols, k % 4, i % 4]

    order = (0, -1, 1, 2)

    def cp_small(h, d):
        v = xv(h, None, big[h], small[h])
        n = 0 if d == 1 else 1
        return remote(v, v, sm_s.at[h, n], sm_r.at[h, n], small_dev(h, d))

    def cp_small_fwd(h, d):
        n, j = (2, 0) if d == 1 else (3, 1)
        v = xv(h, j, big[h], small[h] - d + 4)
        return remote(v, v, sm_s.at[h, n], sm_r.at[h, n], small_dev(h, d))

    def cp_big(h, d, r):
        n = 0 if d == 1 else 1
        v = xv(h, None, big[h], small[h] + order[r] + 4)
        return remote(v, v, bg_s.at[h, n, r], bg_r.at[h, n, r], big_dev(h, d))

    def cp_big_fwd(h, d, r):
        n = 0 if d == 1 else 1
        v = xv(h, n, big[h] - d + 4, small[h] + order[r] + 4)
        return remote(v, v, bf_s.at[h, n, r], bf_r.at[h, n, r], big_dev(h, d))

    def cp_cross(h, d):
        i = (big[h] + d + 4) % 4
        cols = pl.ds(2 * h, 2)
        v = xs.at[g, cols, i] if h == 0 else xs.at[g, cols, :, i]
        return remote(v, v, cx_s.at[h, d % 4], cx_r.at[h, d % 4], sib)

    m_s[...] = jnp.full_like(m_s, -1e30)
    l_s[...] = jnp.zeros_like(l_s)
    acc_s[...] = jnp.zeros_like(acc_s)

    def absorb(k, diagonal):
        there = c - k
        keys = ka[there // 4, there % 4, pl.ds(0, 256), :]
        vals = va[there // 4, there % 4]
        docs = ka[there // 4, there % 4, pl.ds(256, 16), :].astype(F32)
        doc_row = jnp.concatenate([docs[0:1, :], docs[1:2, :]], axis=1)
        doc_col = jnp.broadcast_to(doc_row, (128, 256)).T
        allowed = jnp.concatenate([doc_col, doc_col], axis=1) == docr_ref[0:1, :]
        if diagonal:
            allowed = allowed & (iota((256, 256), 0) <= iota((256, 256), 1))
        bias = jnp.where(allowed, 0.0, -1e30)
        vals_t = vals.astype(F32).T.astype(BF16)
        for h in range(8):
            s = dot_nt(keys, q_ref[:, h * 128 : h * 128 + 128]) + bias
            st = st_ref[h : h + 1, :]
            old = m_s[h : h + 1, :]
            new = jnp.maximum(old, jnp.max(s, axis=0, keepdims=True))
            p = jnp.exp2((s - new) * st)
            fade = jnp.exp2((old - new) * st)
            l_s[h : h + 1, :] = l_s[h : h + 1, :] * fade + jnp.sum(p, axis=0, keepdims=True)
            acc_s[h] = acc_s[h] * fade + dot(vals_t, p.astype(BF16))
            m_s[h : h + 1, :] = new

    def absorb_range(lo, hi):
        def body(k, carry):
            absorb(k, False)
            return carry

        lax.fori_loop(lo, jnp.maximum(jnp.minimum(c + 1, hi), lo), body, 0)

    for h in range(2):
        for d in (1, -1):
            go(cp_small(h, d))
    for h in range(2):
        for d in (1, -1):
            go(cp_big(h, d, 0))

    head_inside(0)
    head_inside(1)

    for d, r in ((1, 1), (-1, 2)):
        for h in range(2):
            cp_small(h, d).wait_recv()
            go(cp_small_fwd(h, d))
            for e in (1, -1):
                go(cp_big(h, e, r))
    for h in range(2):
        for d in (1, -1):
            k_small(h, d).wait_recv()
            go(k_small_fwd(h, d), k_sends)
    heads_in[3].wait()
    absorb(0, True)
    for h in range(2):
        for d in (1, -1):
            cp_small_fwd(h, d).wait_recv()
        for e in (1, -1):
            go(cp_big(h, e, 3))
        go(cp_cross(h, 0))

    def pass_on(r):
        for h in range(2):
            for d in (1, -1):
                cp_big(h, d, r).wait_recv()
                go(cp_big_fwd(h, d, r))

    head_inside(2)
    pass_on(0)
    for h in range(2):
        for d in (1, -1):
            k_small_fwd(h, d).wait_recv()
    head_inside(3)
    head_inside(4)
    pass_on(1)
    pass_on(2)
    head_inside(5)
    head_inside(6)
    head_inside(7)
    pass_on(3)
    for h in range(2):
        go(cp_cross(h, -1))
        go(cp_cross(h, 1))
    for h in range(2):
        for d in (1, -1):
            go(k_big(h, d), k_sends)
    mine.wait()

    def scan(i, carry):
        state, before = carry

        @pl.when(i != c)
        def _():
            k = (c - i + 16) % 16
            remote(
                sb.at[c], sl.at[i], sa_s.at[k], sa_r.at[k], ctx(c + 1)
            ).wait_recv()

        info = sl[i, pl.ds(128, 16), :].astype(F32)
        entering = jnp.where(before == info[2:3, :], state, 0.0)
        en[i] = entering.astype(BF16)
        state = (info[0:1, :] + info[1:2, :]) * entering + sl[i, pl.ds(0, 128), :].astype(F32)
        return state, info[3:4, :]

    lax.fori_loop(
        0, 16, scan, (jnp.zeros((128, 128), F32), jnp.full((1, 128), -1.0, F32))
    )

    def state_back(k):
        return remote(en.at[(c + k) % 16], er.at[c], se_s.at[k], se_r.at[k], ctx(c + k))

    backs = []
    for k in range(1, 16):
        go(state_back(k), backs)
    mine_back = pltpu.make_async_copy(en.at[c], er.at[c], own_sem.at[3])
    mine_back.start()

    for h in range(2):
        for r in range(4):
            for d in (1, -1):
                cp_big_fwd(h, d, r).wait_recv()
        go(cp_cross(h, 2))
    for load in loads:
        load.wait()
    gu[...] = jnp.zeros_like(gu)

    def gate_up(i, carry):
        gg, xx = (i // 4 + g) % 2, i % 4
        block = pl.multiple_of((xx * 2 + gg) * 1024, 1024)
        gu[...] += dot(xs[gg, xx].reshape(512, 1024), wgu[pl.ds(block, 1024), :])
        return carry

    lax.fori_loop(0, 4, gate_up, 0)
    for h in range(2):
        for d in (1, -1):
            k_big(h, d).wait_recv()
            go(k_big_fwd(h, d), k_sends)
    def cross_in(h, d):
        i = (big[h] + d + 4) % 4
        cols = pl.ds(2 * h, 2)
        v = xs.at[1 - g, cols, i] if h == 0 else xs.at[1 - g, cols, :, i]
        return remote(v, v, cx_s.at[h, d % 4], cx_r.at[h, d % 4], sib)

    for h in range(2):
        for d in (0, -1, 1, 2):
            cross_in(h, d).wait_recv()
    lax.fori_loop(4, 8, gate_up, 0)
    gate, up = gu[:, 0:384], gu[:, 384:768]
    hid[...] = (gate / (1.0 + jnp.exp(-gate)) * up).astype(BF16)

    for cp in sends:
        cp.wait_send()
    ps, pa = xs.at[0], xs.at[1]

    def cp_down(xx):
        return remote(ps.at[xx], pl_land.at[xx], cd_s.at[xx], cd_r.at[xx], sib)

    for xx in (0, 2, 1, 3):

        def down_sib(n, carry):
            off = pl.multiple_of(n * 512, 512)
            col = pl.multiple_of((xx * 2 + 1 - g) * 1024 + n * 512, 512)
            r = dot(hid[...], wd[:, pl.ds(col, 512)])
            ps[xx, :, :, :, pl.ds(off, 512)] = r.astype(BF16).reshape(4, 4, CAP, 512)
            return carry

        lax.fori_loop(0, 2, down_sib, 0)
        cp_down(xx).start()

    def pv(h, j, i):
        return pa.at[2 * h + j, i % 4] if h == 0 else pa.at[2 * h + j, :, i % 4]

    def ra_first(h, j):
        d = 1 if j == 0 else -1
        return remote(
            pv(h, j, big[h] + 2), l1.at[h, j], ra_s.at[h, j], ra_r.at[h, j], big_dev(h, d)
        )

    def ra_block(h, j, d):
        n = 0 if d == 1 else 1
        return remote(
            pv(h, j, big[h] + d + 4),
            l2.at[h, n, j],
            ra_s.at[h, 2 + 2 * n + j],
            ra_r.at[h, 2 + 2 * n + j],
            big_dev(h, d),
        )

    for xx in (0, 2, 1, 3):
        cp_down(xx).wait_recv()

        def down_own(n, carry):
            off = pl.multiple_of(n * 512, 512)
            col = pl.multiple_of((xx * 2 + g) * 1024 + n * 512, 512)
            r = dot(hid[...], wd[:, pl.ds(col, 512)])
            r = r.reshape(4, 4, CAP, 512) + pl_land[xx, :, :, :, pl.ds(off, 512)].astype(F32)
            pa[xx, :, :, :, pl.ds(off, 512)] = r.astype(BF16)
            return carry

        lax.fori_loop(0, 2, down_own, 0)
        h, j = xx // 2, xx % 2
        ra_first(h, j).start()
        ra_block(h, j, -1 if j == 0 else 1).start()


    for h in range(2):
        for d in (1, -1):
            k_big_fwd(h, d).wait_recv()
    def add_first(h, j):
        d = 1 if j == 0 else -1
        ra_first(h, j).wait_recv()
        v = pv(h, j, big[h] + d + 4)
        v[...] = (v[...].astype(F32) + l1[h, j].astype(F32)).astype(BF16)
        ra_block(h, j, d).start()

    add_first(0, 0)
    add_first(1, 0)
    absorb_range(1, 4)
    add_first(0, 1)
    add_first(1, 1)
    absorb_range(4, 7)

    def rb_first(h, j):
        d = 1 if j == 0 else -1
        return remote(
            qs.at[h, j, (small[h] + 2) % 4],
            l3.at[h, j],
            rb_s.at[h, j],
            rb_r.at[h, j],
            small_dev(h, d),
        )

    def rb_block(h, j, d):
        n = 0 if d == 1 else 1
        return remote(
            qs.at[h, j, (small[h] + d + 4) % 4],
            l4.at[h, n, j],
            rb_s.at[h, 2 + 2 * n + j],
            rb_r.at[h, 2 + 2 * n + j],
            small_dev(h, d),
        )

    for h in range(2):
        for j in range(2):
            for d in (1, -1):
                ra_block(h, j, d).wait_recv()
            qs[h, j] = (
                pv(h, j, big[h])[...].astype(F32)
                + l2[h, 0, j].astype(F32)
                + l2[h, 1, j].astype(F32)
            ).astype(BF16)
            rb_first(h, j).start()
            rb_block(h, j, -1 if j == 0 else 1).start()


    absorb_range(7, 9)

    for h in range(2):
        for j, d in ((0, 1), (1, -1)):
            rb_first(h, j).wait_recv()
            v = qs.at[h, j, (small[h] + d + 4) % 4]
            v[...] = (v[...].astype(F32) + l3[h, j].astype(F32)).astype(BF16)
            rb_block(h, j, d).start()

    for h in range(8):
        attn_out[:, h * 128 : h * 128 + 128] = (acc_s[h] / l_s[h : h + 1, :]).T.astype(BF16)
    attn_done = pltpu.make_async_copy(attn_out, attn_hbm, out_sem.at[0])
    attn_done.start()

    mine_back.wait()
    for cp in backs:
        cp.wait()
    for h in range(8):
        cols = slice(h * 256, (h + 1) * 256)
        e0 = jnp.concatenate([er[2 * h], er[2 * h + 1]], axis=1)
        e1 = (
            joined[h : h + 1, :] * (dec[0][h : h + 1, :] * e0.astype(F32) + t0s[h])
        ).astype(BF16)
        for k, e in ((0, e0), (1, e1)):
            rows = slice(k * SEG, (k + 1) * SEG)
            carried = dot(c_ref[rows, :], e)
            ssd_out[rows, cols] = (ys[rows, cols] + carried * lift[k][:, h : h + 1]).astype(BF16)

    ssd_done = pltpu.make_async_copy(ssd_out, ssd_hbm, out_sem.at[1])
    ssd_done.start()


    share_x = share[pl.ds(pl.multiple_of(x * CAP, CAP), CAP), 0:1]

    def x_back(k):
        return remote(
            rx.at[(x + k) % 4], fin.at[x], xb_s.at[k - 1], xb_r.at[k - 1], xdev(x + k)
        )

    for h in range(2):
        for j in range(2):
            for d in (1, -1):
                rb_block(h, j, d).wait_recv()
            total = (
                qs[h, j, small[h]].astype(F32)
                + l4[h, 0, j].astype(F32)
                + l4[h, 1, j].astype(F32)
            )
            rx[2 * h + j] = (total * share_x).astype(BF16)
    for k in range(1, 4):
        x_back(k).start()
    own_back = pltpu.make_async_copy(rx.at[x], fin.at[x], own_sem.at[4])
    own_back.start()

    own_back.wait()
    for k in range(1, 4):
        x_back(k).wait()
    moe_out[...] = dot(ptt[...].T.astype(BF16), fin[...].reshape(128, 1024)).astype(BF16)

    moe_done = pltpu.make_async_copy(moe_out, moe_hbm, out_sem.at[2])
    moe_done.start()

    for cp in k_sends:
        cp.wait_send()
    for cp in states:
        cp.wait_send()
    for xx in range(4):
        cp_down(xx).wait_send()
    for h in range(2):
        for j in range(2):
            ra_first(h, j).wait_send()
            rb_first(h, j).wait_send()
            for d in (1, -1):
                ra_block(h, j, d).wait_send()
                rb_block(h, j, d).wait_send()
    attn_done.wait()
    ssd_done.wait()
    moe_done.wait()


def settle(*refs):
    sources, results, held, sems = refs[0:3], refs[3:6], refs[6:9], refs[9]
    parts = []
    for i in range(3):
        for p in range(2):
            rows = pl.ds(p * 128, 128)
            into = pltpu.make_async_copy(
                sources[i].at[rows], held[i].at[rows], sems.at[0, i, p]
            )
            back = pltpu.make_async_copy(
                held[i].at[rows], results[i].at[rows], sems.at[1, i, p]
            )
            into.start()
            parts.append((into, back))
    for into, back in parts:
        into.wait()
        back.start()
    for into, back in parts:
        back.wait()


def on_device(
    ssd_x, ssd_b, ssd_c, dt_steps, decay_rate, skip_gain, doc_ids,
    queries, key_rows, values, log_scale,
    moe_in, expert_ids, route_weights, w_gate, w_up, w_down,
):
    positions = ssd_x.shape[0]
    vmem = pl.BlockSpec(memory_space=pltpu.VMEM)
    smem = pl.BlockSpec(memory_space=pltpu.SMEM)
    anyw = pl.BlockSpec(memory_space=pl.ANY)
    dma = pltpu.SemaphoreType.DMA
    shapes = (
        jax.ShapeDtypeStruct((positions, 2048), BF16),
        jax.ShapeDtypeStruct((positions, 1024), BF16),
        jax.ShapeDtypeStruct((positions, 1024), BF16),
    )
    made = pl.pallas_call(
        kernel,
        out_shape=shapes,
        in_specs=[anyw, vmem, vmem, vmem, smem, smem, vmem, anyw, anyw, anyw, smem]
        + [vmem] * 3
        + [anyw] * 3,
        out_specs=(anyw, anyw, anyw),
        scratch_shapes=[
            pltpu.VMEM((256, 2048), BF16),
            pltpu.VMEM((256, 1024), BF16),
            pltpu.VMEM((8, 256), F32),
            pltpu.VMEM((256, 128), F32),
            pltpu.VMEM((8, 256), F32),
            pltpu.VMEM((256, 2048), BF16),
            pltpu.VMEM((256, 1024), BF16),
            pltpu.VMEM((256, 1024), BF16),
            pltpu.VMEM((8192, 768), BF16),
            pltpu.VMEM((384, 8192), BF16),
            pltpu.VMEM((2, 4, 4, 4, CAP, 1024), BF16),
            pltpu.VMEM((4, CAP, 1024), BF16),
            pltpu.VMEM((128, 256), F32),
            pltpu.VMEM((128, 128), F32),
            pltpu.VMEM((4, 4, 4, CAP, 1024), BF16),
            pltpu.VMEM((2, 2, 4, CAP, 1024), BF16),
            pltpu.VMEM((2, 2, 2, 4, CAP, 1024), BF16),
            pltpu.VMEM((2, 2, 4, CAP, 1024), BF16),
            pltpu.VMEM((2, 2, CAP, 1024), BF16),
            pltpu.VMEM((2, 2, 2, CAP, 1024), BF16),
            pltpu.VMEM((4, CAP, 1024), BF16),
            pltpu.VMEM((4, CAP, 1024), BF16),
            pltpu.VMEM((512, 768), F32),
            pltpu.VMEM((512, 384), BF16),
            pltpu.VMEM((4, 4, 272, 128), BF16),
            pltpu.VMEM((4, 4, 256, 128), BF16),
            pltpu.VMEM((16, 144, 128), BF16),
            pltpu.VMEM((16, 144, 128), BF16),
            pltpu.VMEM((16, 128, 128), BF16),
            pltpu.VMEM((16, 128, 128), BF16),
            pltpu.VMEM((8, 128, 256), F32),
            pltpu.VMEM((256, 2048), F32),
            pltpu.VMEM((8, 256), F32),
            pltpu.VMEM((8, 256), F32),
            pltpu.VMEM((8, 128, 256), F32),
            dma((3,)),
            dma((8,)),
            dma((3,)), dma((3,)),
            dma((2, 4)), dma((2, 4)),
            dma((2, 2, 4)), dma((2, 2, 4)),
            dma((2, 2, 4)), dma((2, 2, 4)),
            dma((2, 4)), dma((2, 4)),
            dma((4,)), dma((4,)),
            dma((2, 6)), dma((2, 6)),
            dma((2, 6)), dma((2, 6)),
            dma((3,)), dma((3,)),
            dma((2, 8)), dma((2, 8)),
            dma((3,)),
            dma((16,)), dma((16,)),
            dma((16,)), dma((16,)),
        ],
        compiler_params=pltpu.CompilerParams(
            collective_id=0, has_side_effects=True, vmem_limit_bytes=60 * 2**20
        ),
        name="layer_pair",
    )(
        ssd_x, ssd_b, ssd_c, dt_steps, decay_rate, skip_gain, doc_ids[None, :],
        queries, key_rows, values, log_scale,
        moe_in, expert_ids.T, route_weights.T, w_gate, w_up, w_down,
    )
    return pl.pallas_call(
        settle,
        out_shape=shapes,
        in_specs=[anyw] * 3,
        out_specs=(anyw, anyw, anyw),
        scratch_shapes=[
            pltpu.VMEM((256, 2048), BF16),
            pltpu.VMEM((256, 1024), BF16),
            pltpu.VMEM((256, 1024), BF16),
            dma((2, 3, 2)),
        ],
        compiler_params=pltpu.CompilerParams(vmem_limit_bytes=60 * 2**20),
        name="settle",
    )(*made)


def solution(mesh):
    in_specs = (
        P("ctx", "mp"),
        P("ctx", None),
        P("ctx", None),
        P("mp", "ctx"),
        P("mp"),
        P("mp"),
        P("ctx"),
        P("ctx", "mp"),
        P("ctx", "mp"),
        P("ctx", "mp"),
        P("mp"),
        P("ctx", "mp"),
        P("ctx", None),
        P("ctx", None),
        P("mp", None, "ctx"),
        P("mp", None, "ctx"),
        P("mp", "ctx", None),
    )
    out_specs = (P("ctx", "mp"), P("ctx", "mp"), P("ctx", "mp"))
    return jax.shard_map(
        on_device, mesh=mesh, in_specs=in_specs, out_specs=out_specs, check_vma=False
    )
```

```python
import math

import jax
import jax.numpy as jnp
from jax import lax
from jax.experimental import pallas as pl
from jax.experimental.pallas import tpu as pltpu
from jax.sharding import PartitionSpec as P

HEAD_DIM = 128
HELD = 4
SEG = 128
CAP = 32
LOG2E = math.log2(math.e)
MESH = pl.DeviceIdType.MESH
F32 = jnp.float32
BF16 = jnp.bfloat16
HIGH = lax.Precision.HIGHEST


def dot(a, b, precision=None):
    return jnp.dot(a, b, preferred_element_type=F32, precision=precision)


def dot_nt(a, b, precision=None):
    return lax.dot_general(
        a, b, (((1,), (1,)), ((), ())), preferred_element_type=F32, precision=precision
    )


def iota(shape, dim):
    return lax.broadcasted_iota(jnp.int32, shape, dim)


def kernel(
    x_hbm, b_ref, c_ref, dt_ref, rate_ref, skip_ref, doc_ref, q_hbm, key_ref, val_ref, scale_ref,
    moe_ref, ids_ref, rw_ref, wg_ref, wu_ref, wd_ref,
    ssd_hbm, attn_hbm, moe_hbm,
    x_ref, q_ref, docr_ref, docc_ref, st_ref, ssd_out, attn_out, moe_out,
    wgu, wd, xs, pk, ptt, share, pl_land, l1, l2, qs, l3, l4, rx, fin, gu, hid,
    ka, va, sb, sl, en, er, t0s, ys, m_s, l_s, acc_s,
    w_sem, own_sem,
    xa_s, xa_r, sm_s, sm_r, bg_s, bg_r, bf_s, bf_r, cx_s, cx_r,
    cd_s, cd_r, ra_s, ra_r, rb_s, rb_r, xb_s, xb_r,
    ks_s, ks_r, out_sem, sa_s, sa_r, se_s, se_r,
):
    c = lax.axis_index("ctx")
    m = lax.axis_index("mp")
    z, y = c // 4, c % 4
    x, g = m // 2, m % 2
    sib = {"ctx": c, "mp": x * 2 + (1 - g)}

    def zy(zz, yy):
        return {"ctx": (zz % 4) * 4 + yy % 4, "mp": m}

    def xdev(xx):
        return {"ctx": c, "mp": (xx % 4) * 2 + g}

    def ctx(cc):
        return {"ctx": cc % 16, "mp": m}

    def remote(src, dst, s, r, dev):
        return pltpu.make_async_remote_copy(
            src_ref=src, dst_ref=dst, send_sem=s, recv_sem=r, device_id=dev, device_id_type=MESH
        )

    loads = [
        pltpu.make_async_copy(wg_ref.at[0], wgu.at[:, pl.ds(0, 384)], w_sem.at[0]),
        pltpu.make_async_copy(wu_ref.at[0], wgu.at[:, pl.ds(384, 384)], w_sem.at[1]),
        pltpu.make_async_copy(wd_ref.at[0], wd, w_sem.at[2]),
    ]
    heads_in = [
        pltpu.make_async_copy(key_ref, ka.at[z, y, pl.ds(0, 256)], own_sem.at[1]),
        pltpu.make_async_copy(val_ref, va.at[z, y], own_sem.at[5]),
        pltpu.make_async_copy(x_hbm, x_ref, own_sem.at[6]),
        pltpu.make_async_copy(q_hbm, q_ref, own_sem.at[7]),
    ]
    for load in heads_in + loads:
        load.start()

    bar = pltpu.get_barrier_semaphore()
    for k in range(1, 16):
        pl.semaphore_signal(bar, inc=1, device_id=ctx(c + k), device_id_type=MESH)
    for k in range(1, 4):
        pl.semaphore_signal(bar, inc=1, device_id=xdev(x + k), device_id_type=MESH)
    pl.semaphore_signal(bar, inc=1, device_id=sib, device_id_type=MESH)

    docs = doc_ref[...].astype(F32)
    docr_ref[...] = jnp.broadcast_to(docs, (8, 256))
    docc_ref[...] = jnp.broadcast_to(docs, (128, 256)).T
    ka[z, y, pl.ds(256, 16), :] = jnp.where(
        iota((16, 128), 0) == 0, docs[:, 0:128], docs[:, 128:256]
    ).astype(BF16)
    growth = jnp.log((c * 256 + 1 + iota((8, 256), 1)).astype(F32))
    slope = jnp.zeros((8, 256), F32)
    for h in range(8):
        slope = jnp.where(iota((8, 256), 0) == h, scale_ref[h], slope)
    st_ref[...] = (1.0 + slope * growth) * (LOG2E / math.sqrt(HEAD_DIM))

    expert = iota((8, 256), 0)
    ids0, ids1 = ids_ref[0:1, :], ids_ref[1:2, :]
    named = ((ids0 == expert) | (ids1 == expert)).astype(F32)
    weight = jnp.where(ids0 == expert, rw_ref[0:1, :], 0.0) + jnp.where(
        ids1 == expert, rw_ref[1:2, :], 0.0
    )
    upto = (iota((256, 256), 0) <= iota((256, 256), 1)).astype(BF16)
    rank = dot(named.astype(BF16), upto).astype(jnp.int32) - 1
    slot = iota((CAP, 256), 0)
    for e in range(HELD):
        place = jnp.where((rank[e : e + 1, :] == slot) & (named[e : e + 1, :] > 0.0), 1.0, 0.0)
        pk[e] = dot(place.astype(BF16), moe_ref[...]).astype(BF16)
        share[pl.ds(e * CAP, CAP), :] = jnp.broadcast_to(
            jnp.sum(place * weight[e : e + 1, :], axis=1, keepdims=True), (CAP, 128)
        )
        ptt[pl.ds(e * CAP, CAP), :] = place

    pl.semaphore_wait(bar, 19)

    xa = []
    for k in range(1, 4):
        cp = remote(
            pk.at[(x + k) % 4], xs.at[g, x, z, y], xa_s.at[k - 1], xa_r.at[k - 1], xdev(x + k)
        )
        cp.start()
        xa.append(cp)
    own = pltpu.make_async_copy(pk.at[x], xs.at[g, x, z, y], own_sem.at[0])
    own.start()
    big = (z, y)
    small = (y, z)

    def big_dev(h, d):
        return zy(z + d, y) if h == 0 else zy(z, y + d)

    def small_dev(h, d):
        return zy(z, y + d) if h == 0 else zy(z + d, y)

    key_rows = ((0, 144), (144, 128)), ((0, 128), (128, 128))

    def kcp(h, n, i, k, j, dev):
        arr = (ka, va)[h]
        rows = pl.ds(*key_rows[h][j]) if j is not None else slice(None)
        if k is None:
            v = arr.at[i % 4, :, rows] if h == 0 else arr.at[:, i % 4, rows]
        else:
            v = arr.at[i % 4, k % 4, rows] if h == 0 else arr.at[k % 4, i % 4, rows]
        return remote(v, v, ks_s.at[h, n], ks_r.at[h, n], dev)

    def k_small(h, d):
        return kcp(h, 0 if d == 1 else 1, big[h], small[h], None, small_dev(h, d))

    def k_small_fwd(h, d):
        n, j = (2, 0) if d == 1 else (3, 1)
        return kcp(h, n, big[h], small[h] - d + 4, j, small_dev(h, d))

    def k_big(h, d):
        return kcp(h, 4 if d == 1 else 5, big[h], None, None, big_dev(h, d))

    def k_big_fwd(h, d):
        n, j = (6, 0) if d == 1 else (7, 1)
        return kcp(h, n, big[h] - d + 4, None, j, big_dev(h, d))

    sends = []
    k_sends = []

    def go(cp, kept=None):
        cp.start()
        (sends if kept is None else kept).append(cp)

    heads_in[0].wait()
    heads_in[1].wait()
    for h in range(2):
        for d in (1, -1):
            go(k_small(h, d), k_sends)
    heads_in[2].wait()

    low = iota((SEG, SEG), 0) >= iota((SEG, SEG), 1)
    tri = low.astype(F32)
    cum_r, cum_c, inner, linked, bt = [], [], [], [], []
    rate = jnp.zeros((8, 1), F32)
    for h in range(8):
        rate = jnp.where(iota((8, 1), 0) == h, rate_ref[h], rate)
    for k in range(2):
        rows = slice(k * SEG, (k + 1) * SEG)
        ld = -(dt_ref[:, rows] * rate)
        cum_r.append(dot_nt(ld, tri, HIGH))
        cum_c.append(dot_nt(tri, ld, HIGH))
        inner.append(dot_nt(c_ref[rows, :], b_ref[rows, :]))
        linked.append((docc_ref[rows, :] == docr_ref[0:1, rows]) & low)
        bt.append(b_ref[rows, :].astype(F32).T)
    first = [docr_ref[:, k * SEG : k * SEG + 1] for k in range(2)]
    last = [docr_ref[:, k * SEG + SEG - 1 : (k + 1) * SEG] for k in range(2)]
    dec = [
        jnp.exp(cum_r[k][:, SEG - 1 : SEG]) * (first[k] == last[k]).astype(F32) for k in range(2)
    ]
    tail = [
        jnp.where(
            docr_ref[:, k * SEG : (k + 1) * SEG] == last[k],
            jnp.exp(cum_r[k][:, SEG - 1 : SEG] - cum_r[k]),
            0.0,
        )
        for k in range(2)
    ]
    lift = [
        jnp.exp(cum_c[k])
        * (docc_ref[k * SEG : (k + 1) * SEG, 0:8] == first[k][0:1, :]).astype(F32)
        for k in range(2)
    ]
    joined = (last[0] == first[1]).astype(F32)
    whole = dec[1] * joined * dec[0]

    def head_states(h):
        cols = slice(h * 256, (h + 1) * 256)
        locs = []
        for k in range(2):
            rows = slice(k * SEG, (k + 1) * SEG)
            xb = x_ref[rows, cols]
            locs.append(dot((bt[k] * tail[k][h : h + 1, :]).astype(BF16), xb))
        t0s[h] = locs[0]
        total = locs[1] + (dec[1] * joined)[h : h + 1, :] * locs[0]
        row = iota((16, 128), 0)
        w = jnp.broadcast_to(whole[h : h + 1, :], (16, 128))
        w_hi = w.astype(BF16).astype(F32)
        info = jnp.where(
            row == 0,
            w_hi,
            jnp.where(
                row == 1,
                w - w_hi,
                jnp.where(row == 2, first[0][0:1, :], last[1][0:1, :]),
            ),
        ).astype(BF16)
        for half in range(2):
            sb[2 * h + half, pl.ds(0, 128), :] = total[:, half * 128 : half * 128 + 128].astype(
                BF16
            )
            sb[2 * h + half, pl.ds(128, 16), :] = info

    def head_inside(h):
        cols = slice(h * 256, (h + 1) * 256)
        for k in range(2):
            rows = slice(k * SEG, (k + 1) * SEG)
            xb = x_ref[rows, cols]
            gap = cum_c[k][:, h : h + 1] - cum_r[k][h : h + 1, :]
            w = jnp.where(linked[k], inner[k] * jnp.exp(jnp.where(linked[k], gap, 0.0)), 0.0)
            ys[rows, cols] = dot(w.astype(BF16), xb) + skip_ref[h] * xb.astype(F32)

    for h in range(8):
        head_states(h)

    def state_out(k):
        return remote(sb.at[(c + k) % 16], sl.at[c], sa_s.at[k], sa_r.at[k], ctx(c + k))

    states = []
    for k in range(1, 16):
        go(state_out(k), states)
    mine = pltpu.make_async_copy(sb.at[c], sl.at[c], own_sem.at[2])
    mine.start()

    own.wait()
    for cp in xa:
        cp.wait()

    def xv(h, j, i, k):
        cols = pl.ds(2 * h, 2) if j is None else 2 * h + j
        return xs.at[g, cols, i % 4, k % 4] if h == 0 else xs.at[g, cols, k % 4, i % 4]

    order = (0, -1, 1, 2)

    def cp_small(h, d):
        v = xv(h, None, big[h], small[h])
        n = 0 if d == 1 else 1
        return remote(v, v, sm_s.at[h, n], sm_r.at[h, n], small_dev(h, d))

    def cp_small_fwd(h, d):
        n, j = (2, 0) if d == 1 else (3, 1)
        v = xv(h, j, big[h], small[h] - d + 4)
        return remote(v, v, sm_s.at[h, n], sm_r.at[h, n], small_dev(h, d))

    def cp_big(h, d, r):
        n = 0 if d == 1 else 1
        v = xv(h, None, big[h], small[h] + order[r] + 4)
        return remote(v, v, bg_s.at[h, n, r], bg_r.at[h, n, r], big_dev(h, d))

    def cp_big_fwd(h, d, r):
        n = 0 if d == 1 else 1
        v = xv(h, n, big[h] - d + 4, small[h] + order[r] + 4)
        return remote(v, v, bf_s.at[h, n, r], bf_r.at[h, n, r], big_dev(h, d))

    def cp_cross(h, d):
        i = (big[h] + d + 4) % 4
        cols = pl.ds(2 * h, 2)
        v = xs.at[g, cols, i] if h == 0 else xs.at[g, cols, :, i]
        return remote(v, v, cx_s.at[h, d % 4], cx_r.at[h, d % 4], sib)

    m_s[...] = jnp.full_like(m_s, -1e30)
    l_s[...] = jnp.zeros_like(l_s)
    acc_s[...] = jnp.zeros_like(acc_s)

    def absorb(k, diagonal):
        there = c - k
        keys = ka[there // 4, there % 4, pl.ds(0, 256), :]
        vals = va[there // 4, there % 4]
        docs = ka[there // 4, there % 4, pl.ds(256, 16), :].astype(F32)
        doc_row = jnp.concatenate([docs[0:1, :], docs[1:2, :]], axis=1)
        doc_col = jnp.broadcast_to(doc_row, (128, 256)).T
        allowed = jnp.concatenate([doc_col, doc_col], axis=1) == docr_ref[0:1, :]
        if diagonal:
            allowed = allowed & (iota((256, 256), 0) <= iota((256, 256), 1))
        bias = jnp.where(allowed, 0.0, -1e30)
        vals_t = vals.astype(F32).T.astype(BF16)
        for h in range(8):
            s = dot_nt(keys, q_ref[:, h * 128 : h * 128 + 128]) + bias
            st = st_ref[h : h + 1, :]
            old = m_s[h : h + 1, :]
            new = jnp.maximum(old, jnp.max(s, axis=0, keepdims=True))
            p = jnp.exp2((s - new) * st)
            fade = jnp.exp2((old - new) * st)
            l_s[h : h + 1, :] = l_s[h : h + 1, :] * fade + jnp.sum(p, axis=0, keepdims=True)
            acc_s[h] = acc_s[h] * fade + dot(vals_t, p.astype(BF16))
            m_s[h : h + 1, :] = new

    def absorb_range(lo, hi):
        def body(k, carry):
            absorb(k, False)
            return carry

        lax.fori_loop(lo, jnp.maximum(jnp.minimum(c + 1, hi), lo), body, 0)

    for h in range(2):
        for d in (1, -1):
            go(cp_small(h, d))
    for h in range(2):
        for d in (1, -1):
            go(cp_big(h, d, 0))

    head_inside(0)
    head_inside(1)

    for d, r in ((1, 1), (-1, 2)):
        for h in range(2):
            cp_small(h, d).wait_recv()
            go(cp_small_fwd(h, d))
            for e in (1, -1):
                go(cp_big(h, e, r))
    for h in range(2):
        for d in (1, -1):
            k_small(h, d).wait_recv()
            go(k_small_fwd(h, d), k_sends)
    heads_in[3].wait()
    absorb(0, True)
    for h in range(2):
        for d in (1, -1):
            cp_small_fwd(h, d).wait_recv()
        for e in (1, -1):
            go(cp_big(h, e, 3))
        go(cp_cross(h, 0))

    def pass_on(r):
        for h in range(2):
            for d in (1, -1):
                cp_big(h, d, r).wait_recv()
                go(cp_big_fwd(h, d, r))

    head_inside(2)
    pass_on(0)
    for h in range(2):
        for d in (1, -1):
            k_small_fwd(h, d).wait_recv()
    head_inside(3)
    head_inside(4)
    pass_on(1)
    pass_on(2)
    head_inside(5)
    head_inside(6)
    head_inside(7)
    pass_on(3)
    for h in range(2):
        go(cp_cross(h, -1))
        go(cp_cross(h, 1))
    for h in range(2):
        for d in (1, -1):
            go(k_big(h, d), k_sends)
    mine.wait()

    def scan(i, carry):
        state, before = carry

        @pl.when(i != c)
        def _():
            k = (c - i + 16) % 16
            remote(
                sb.at[c], sl.at[i], sa_s.at[k], sa_r.at[k], ctx(c + 1)
            ).wait_recv()

        info = sl[i, pl.ds(128, 16), :].astype(F32)
        entering = jnp.where(before == info[2:3, :], state, 0.0)
        en[i] = entering.astype(BF16)
        state = (info[0:1, :] + info[1:2, :]) * entering + sl[i, pl.ds(0, 128), :].astype(F32)
        return state, info[3:4, :]

    lax.fori_loop(
        0, 16, scan, (jnp.zeros((128, 128), F32), jnp.full((1, 128), -1.0, F32))
    )

    def state_back(k):
        return remote(en.at[(c + k) % 16], er.at[c], se_s.at[k], se_r.at[k], ctx(c + k))

    backs = []
    for k in range(1, 16):
        go(state_back(k), backs)
    mine_back = pltpu.make_async_copy(en.at[c], er.at[c], own_sem.at[3])
    mine_back.start()

    for h in range(2):
        for r in range(4):
            for d in (1, -1):
                cp_big_fwd(h, d, r).wait_recv()
        go(cp_cross(h, 2))
    for load in loads:
        load.wait()
    gu[...] = jnp.zeros_like(gu)

    def gate_up(i, carry):
        gg, xx = (i // 4 + g) % 2, i % 4
        block = pl.multiple_of((xx * 2 + gg) * 1024, 1024)
        gu[...] += dot(xs[gg, xx].reshape(512, 1024), wgu[pl.ds(block, 1024), :])
        return carry

    lax.fori_loop(0, 4, gate_up, 0)
    for h in range(2):
        for d in (1, -1):
            k_big(h, d).wait_recv()
            go(k_big_fwd(h, d), k_sends)
    def cross_in(h, d):
        i = (big[h] + d + 4) % 4
        cols = pl.ds(2 * h, 2)
        v = xs.at[1 - g, cols, i] if h == 0 else xs.at[1 - g, cols, :, i]
        return remote(v, v, cx_s.at[h, d % 4], cx_r.at[h, d % 4], sib)

    for h in range(2):
        for d in (0, -1, 1, 2):
            cross_in(h, d).wait_recv()
    lax.fori_loop(4, 8, gate_up, 0)
    gate, up = gu[:, 0:384], gu[:, 384:768]
    hid[...] = (gate / (1.0 + jnp.exp(-gate)) * up).astype(BF16)

    for cp in sends:
        cp.wait_send()
    ps, pa = xs.at[0], xs.at[1]

    def cp_down(xx):
        return remote(ps.at[xx], pl_land.at[xx], cd_s.at[xx], cd_r.at[xx], sib)

    for xx in (0, 2, 1, 3):

        def down_sib(n, carry):
            off = pl.multiple_of(n * 512, 512)
            col = pl.multiple_of((xx * 2 + 1 - g) * 1024 + n * 512, 512)
            r = dot(hid[...], wd[:, pl.ds(col, 512)])
            ps[xx, :, :, :, pl.ds(off, 512)] = r.astype(BF16).reshape(4, 4, CAP, 512)
            return carry

        lax.fori_loop(0, 2, down_sib, 0)
        cp_down(xx).start()

    def pv(h, j, i):
        return pa.at[2 * h + j, i % 4] if h == 0 else pa.at[2 * h + j, :, i % 4]

    def ra_first(h, j):
        d = 1 if j == 0 else -1
        return remote(
            pv(h, j, big[h] + 2), l1.at[h, j], ra_s.at[h, j], ra_r.at[h, j], big_dev(h, d)
        )

    def ra_block(h, j, d):
        n = 0 if d == 1 else 1
        return remote(
            pv(h, j, big[h] + d + 4),
            l2.at[h, n, j],
            ra_s.at[h, 2 + 2 * n + j],
            ra_r.at[h, 2 + 2 * n + j],
            big_dev(h, d),
        )

    for xx in (0, 2, 1, 3):
        cp_down(xx).wait_recv()

        def down_own(n, carry):
            off = pl.multiple_of(n * 512, 512)
            col = pl.multiple_of((xx * 2 + g) * 1024 + n * 512, 512)
            r = dot(hid[...], wd[:, pl.ds(col, 512)])
            r = r.reshape(4, 4, CAP, 512) + pl_land[xx, :, :, :, pl.ds(off, 512)].astype(F32)
            pa[xx, :, :, :, pl.ds(off, 512)] = r.astype(BF16)
            return carry

        lax.fori_loop(0, 2, down_own, 0)
        h, j = xx // 2, xx % 2
        ra_first(h, j).start()
        if j == 1:
            ra_block(h, 0, -1).start()
            ra_block(h, 1, 1).start()


    for h in range(2):
        for d in (1, -1):
            k_big_fwd(h, d).wait_recv()
    def add_first(h, j):
        d = 1 if j == 0 else -1
        ra_first(h, j).wait_recv()
        v = pv(h, j, big[h] + d + 4)
        v[...] = (v[...].astype(F32) + l1[h, j].astype(F32)).astype(BF16)
        ra_block(h, j, d).start()

    add_first(0, 0)
    add_first(1, 0)
    absorb_range(1, 4)
    add_first(0, 1)
    add_first(1, 1)
    absorb_range(4, 7)

    def rb_first(h, j):
        d = 1 if j == 0 else -1
        return remote(
            qs.at[h, j, (small[h] + 2) % 4],
            l3.at[h, j],
            rb_s.at[h, j],
            rb_r.at[h, j],
            small_dev(h, d),
        )

    def rb_block(h, j, d):
        n = 0 if d == 1 else 1
        return remote(
            qs.at[h, j, (small[h] + d + 4) % 4],
            l4.at[h, n, j],
            rb_s.at[h, 2 + 2 * n + j],
            rb_r.at[h, 2 + 2 * n + j],
            small_dev(h, d),
        )

    for h in range(2):
        for j in range(2):
            for d in (1, -1):
                ra_block(h, j, d).wait_recv()
            qs[h, j] = (
                pv(h, j, big[h])[...].astype(F32)
                + l2[h, 0, j].astype(F32)
                + l2[h, 1, j].astype(F32)
            ).astype(BF16)
            rb_first(h, j).start()
            rb_block(h, j, -1 if j == 0 else 1).start()


    absorb_range(7, 9)

    for h in range(2):
        for j, d in ((0, 1), (1, -1)):
            rb_first(h, j).wait_recv()
            v = qs.at[h, j, (small[h] + d + 4) % 4]
            v[...] = (v[...].astype(F32) + l3[h, j].astype(F32)).astype(BF16)
            rb_block(h, j, d).start()

    for h in range(8):
        attn_out[:, h * 128 : h * 128 + 128] = (acc_s[h] / l_s[h : h + 1, :]).T.astype(BF16)
    attn_done = pltpu.make_async_copy(attn_out, attn_hbm, out_sem.at[0])
    attn_done.start()

    mine_back.wait()
    for cp in backs:
        cp.wait()
    for h in range(8):
        cols = slice(h * 256, (h + 1) * 256)
        e0 = jnp.concatenate([er[2 * h], er[2 * h + 1]], axis=1)
        e1 = (
            joined[h : h + 1, :] * (dec[0][h : h + 1, :] * e0.astype(F32) + t0s[h])
        ).astype(BF16)
        for k, e in ((0, e0), (1, e1)):
            rows = slice(k * SEG, (k + 1) * SEG)
            carried = dot(c_ref[rows, :], e)
            ssd_out[rows, cols] = (ys[rows, cols] + carried * lift[k][:, h : h + 1]).astype(BF16)

    ssd_done = pltpu.make_async_copy(ssd_out, ssd_hbm, out_sem.at[1])
    ssd_done.start()


    share_x = share[pl.ds(pl.multiple_of(x * CAP, CAP), CAP), 0:1]

    def x_back(k):
        return remote(
            rx.at[(x + k) % 4], fin.at[x], xb_s.at[k - 1], xb_r.at[k - 1], xdev(x + k)
        )

    for h in range(2):
        for j in range(2):
            for d in (1, -1):
                rb_block(h, j, d).wait_recv()
            total = (
                qs[h, j, small[h]].astype(F32)
                + l4[h, 0, j].astype(F32)
                + l4[h, 1, j].astype(F32)
            )
            rx[2 * h + j] = (total * share_x).astype(BF16)
    for k in range(1, 4):
        x_back(k).start()
    own_back = pltpu.make_async_copy(rx.at[x], fin.at[x], own_sem.at[4])
    own_back.start()

    own_back.wait()
    for k in range(1, 4):
        x_back(k).wait()
    moe_out[...] = dot(ptt[...].T.astype(BF16), fin[...].reshape(128, 1024)).astype(BF16)

    moe_done = pltpu.make_async_copy(moe_out, moe_hbm, out_sem.at[2])
    moe_done.start()

    for cp in k_sends:
        cp.wait_send()
    for cp in states:
        cp.wait_send()
    for xx in range(4):
        cp_down(xx).wait_send()
    for h in range(2):
        for j in range(2):
            ra_first(h, j).wait_send()
            rb_first(h, j).wait_send()
            for d in (1, -1):
                ra_block(h, j, d).wait_send()
                rb_block(h, j, d).wait_send()
    attn_done.wait()
    ssd_done.wait()
    moe_done.wait()


def settle(*refs):
    sources, results, held, sems = refs[0:3], refs[3:6], refs[6:9], refs[9]
    parts = []
    for i in range(3):
        for p in range(2):
            rows = pl.ds(p * 128, 128)
            into = pltpu.make_async_copy(
                sources[i].at[rows], held[i].at[rows], sems.at[0, i, p]
            )
            back = pltpu.make_async_copy(
                held[i].at[rows], results[i].at[rows], sems.at[1, i, p]
            )
            into.start()
            parts.append((into, back))
    for into, back in parts:
        into.wait()
        back.start()
    for into, back in parts:
        back.wait()


def on_device(
    ssd_x, ssd_b, ssd_c, dt_steps, decay_rate, skip_gain, doc_ids,
    queries, key_rows, values, log_scale,
    moe_in, expert_ids, route_weights, w_gate, w_up, w_down,
):
    positions = ssd_x.shape[0]
    vmem = pl.BlockSpec(memory_space=pltpu.VMEM)
    smem = pl.BlockSpec(memory_space=pltpu.SMEM)
    anyw = pl.BlockSpec(memory_space=pl.ANY)
    dma = pltpu.SemaphoreType.DMA
    shapes = (
        jax.ShapeDtypeStruct((positions, 2048), BF16),
        jax.ShapeDtypeStruct((positions, 1024), BF16),
        jax.ShapeDtypeStruct((positions, 1024), BF16),
    )
    made = pl.pallas_call(
        kernel,
        out_shape=shapes,
        in_specs=[anyw, vmem, vmem, vmem, smem, smem, vmem, anyw, anyw, anyw, smem]
        + [vmem] * 3
        + [anyw] * 3,
        out_specs=(anyw, anyw, anyw),
        scratch_shapes=[
            pltpu.VMEM((256, 2048), BF16),
            pltpu.VMEM((256, 1024), BF16),
            pltpu.VMEM((8, 256), F32),
            pltpu.VMEM((256, 128), F32),
            pltpu.VMEM((8, 256), F32),
            pltpu.VMEM((256, 2048), BF16),
            pltpu.VMEM((256, 1024), BF16),
            pltpu.VMEM((256, 1024), BF16),
            pltpu.VMEM((8192, 768), BF16),
            pltpu.VMEM((384, 8192), BF16),
            pltpu.VMEM((2, 4, 4, 4, CAP, 1024), BF16),
            pltpu.VMEM((4, CAP, 1024), BF16),
            pltpu.VMEM((128, 256), F32),
            pltpu.VMEM((128, 128), F32),
            pltpu.VMEM((4, 4, 4, CAP, 1024), BF16),
            pltpu.VMEM((2, 2, 4, CAP, 1024), BF16),
            pltpu.VMEM((2, 2, 2, 4, CAP, 1024), BF16),
            pltpu.VMEM((2, 2, 4, CAP, 1024), BF16),
            pltpu.VMEM((2, 2, CAP, 1024), BF16),
            pltpu.VMEM((2, 2, 2, CAP, 1024), BF16),
            pltpu.VMEM((4, CAP, 1024), BF16),
            pltpu.VMEM((4, CAP, 1024), BF16),
            pltpu.VMEM((512, 768), F32),
            pltpu.VMEM((512, 384), BF16),
            pltpu.VMEM((4, 4, 272, 128), BF16),
            pltpu.VMEM((4, 4, 256, 128), BF16),
            pltpu.VMEM((16, 144, 128), BF16),
            pltpu.VMEM((16, 144, 128), BF16),
            pltpu.VMEM((16, 128, 128), BF16),
            pltpu.VMEM((16, 128, 128), BF16),
            pltpu.VMEM((8, 128, 256), F32),
            pltpu.VMEM((256, 2048), F32),
            pltpu.VMEM((8, 256), F32),
            pltpu.VMEM((8, 256), F32),
            pltpu.VMEM((8, 128, 256), F32),
            dma((3,)),
            dma((8,)),
            dma((3,)), dma((3,)),
            dma((2, 4)), dma((2, 4)),
            dma((2, 2, 4)), dma((2, 2, 4)),
            dma((2, 2, 4)), dma((2, 2, 4)),
            dma((2, 4)), dma((2, 4)),
            dma((4,)), dma((4,)),
            dma((2, 6)), dma((2, 6)),
            dma((2, 6)), dma((2, 6)),
            dma((3,)), dma((3,)),
            dma((2, 8)), dma((2, 8)),
            dma((3,)),
            dma((16,)), dma((16,)),
            dma((16,)), dma((16,)),
        ],
        compiler_params=pltpu.CompilerParams(
            collective_id=0, has_side_effects=True, vmem_limit_bytes=60 * 2**20
        ),
        name="layer_pair",
    )(
        ssd_x, ssd_b, ssd_c, dt_steps, decay_rate, skip_gain, doc_ids[None, :],
        queries, key_rows, values, log_scale,
        moe_in, expert_ids.T, route_weights.T, w_gate, w_up, w_down,
    )
    return pl.pallas_call(
        settle,
        out_shape=shapes,
        in_specs=[anyw] * 3,
        out_specs=(anyw, anyw, anyw),
        scratch_shapes=[
            pltpu.VMEM((256, 2048), BF16),
            pltpu.VMEM((256, 1024), BF16),
            pltpu.VMEM((256, 1024), BF16),
            dma((2, 3, 2)),
        ],
        compiler_params=pltpu.CompilerParams(vmem_limit_bytes=60 * 2**20),
        name="settle",
    )(*made)


def solution(mesh):
    in_specs = (
        P("ctx", "mp"),
        P("ctx", None),
        P("ctx", None),
        P("mp", "ctx"),
        P("mp"),
        P("mp"),
        P("ctx"),
        P("ctx", "mp"),
        P("ctx", "mp"),
        P("ctx", "mp"),
        P("mp"),
        P("ctx", "mp"),
        P("ctx", None),
        P("ctx", None),
        P("mp", None, "ctx"),
        P("mp", None, "ctx"),
        P("mp", "ctx", None),
    )
    out_specs = (P("ctx", "mp"), P("ctx", "mp"), P("ctx", "mp"))
    return jax.shard_map(
        on_device, mesh=mesh, in_specs=in_specs, out_specs=out_specs, check_vma=False
    )
```
